32 devices in a mesh: dp: 8 (over z, y), sp: 4 (over x, core).
Axes of the slice: x: 2, y: 2, z: 4, core: 2. Of those that a mesh axis runs over, the one named last changes fastest.
Arguments:
- tokens: bfloat16 [16, 1536, 2048], P('dp', 'sp'), may hold values from -6 to 6
- cotangent: bfloat16 [16, 1536, 2048], P('dp', 'sp'), may hold values from -6 to 6
- lengths: int32 [16], P('dp'), may hold values from 256 to 1536, as said below
- query_weight: bfloat16 [2048, 2048], P(('dp', 'sp')), may hold values from -0.125 to 0.125
- key_weight: bfloat16 [2048, 256], P(('dp', 'sp')), may hold values from -0.125 to 0.125
- value_weight: bfloat16 [2048, 256], P(('dp', 'sp')), may hold values from -0.125 to 0.125
- output_weight: bfloat16 [2048, 2048], P(('dp', 'sp')), may hold values from -1 to 1
- gate_weight: bfloat16 [2048, 5632], P('dp', 'sp'), may hold values from -0.125 to 0.125
- up_weight: bfloat16 [2048, 5632], P('dp', 'sp'), may hold values from -0.125 to 0.125
- down_weight: bfloat16 [5632, 2048], P('sp', 'dp'), may hold values from -0.078125 to 0.078125
- attention_gain: bfloat16 [2048], P(('dp', 'sp')), may hold values from 0.5 to 1.5
- feed_gain: bfloat16 [2048], P(('dp', 'sp')), may hold values from 0.5 to 1.5
Outputs:
- block_out: bfloat16 [16, 1536, 2048], P('dp', 'sp')
- input_grad: bfloat16 [16, 1536, 2048], P('dp', 'sp')
- query_grad: float32 [2048, 2048], P(('dp', 'sp'))
- key_grad: float32 [2048, 256], P(('dp', 'sp'))
- value_grad: float32 [2048, 256], P(('dp', 'sp'))
- output_grad: float32 [2048, 2048], P(('dp', 'sp'))
- gate_grad: float32 [2048, 5632], P('dp', 'sp')
- up_grad: float32 [2048, 5632], P('dp', 'sp')
- down_grad: float32 [5632, 2048], P('sp', 'dp')
- attention_gain_grad: float32 [2048], P(('dp', 'sp'))
- feed_gain_grad: float32 [2048], P(('dp', 'sp'))
- branch_norms: float32 [3, 16], P(None, 'dp')
The draws below stay inside these ranges and needn't reach their ends.
Inputs may be any that keep to these rules, and one draw needn't show every extreme that they name: `lengths`: among the 2 sequences of each index of dp, one drawn at random is exactly 1536 long.
All inputs are finite; a program needn't handle non-finite values.
Results may differ from the reference program's by a relative error of at most 0.017.
Values may be sent and summed in bfloat16 or wider, within the bound.
No kernel may reach another device: no remote copies, remote signals or barrier semaphores. Data moves between devices by JAX's collectives and lax.ppermute only.
A program may use at most 320 MiB of HBM per device.

```python
import jax
import jax.numpy as jnp
from jax import lax

D = 2048
HEADS = 32
KV = 4
HD = 64
FF = 5632
SEQ_LEN = 1536
SEQ_DEV = 2
SEQS = 16


def draw_lengths(key, part):
    key = jax.random.fold_in(key, 7)
    first_key, second_key = jax.random.split(key)
    drawn_lengths = jax.random.randint(first_key, (SEQS,), SEQ_LEN // 6, SEQ_LEN + 1)
    chosen = jax.random.randint(second_key, (SEQS // SEQ_DEV,), 0, SEQ_DEV)
    slot_rank = jnp.arange(SEQS) % SEQ_DEV
    full_rows = slot_rank == jnp.repeat(chosen, SEQ_DEV)
    return jnp.where(full_rows, SEQ_LEN, drawn_lengths).astype(jnp.int32)


def levels(stream_key, shape, pieces, least, largest):
    loudness = 1.0
    for position, blocks in pieces:
        draws = jax.random.uniform(jax.random.fold_in(jax.random.fold_in(stream_key, 6), position), (blocks,), jnp.float32, least / len(pieces), largest / len(pieces))
        loudness = loudness * jnp.repeat(jnp.exp(draws), shape[position] // blocks).reshape((-1,) + (1,) * (len(shape) - 1 - position))
    return loudness


def bell_draw(stream_key, extent, spread, limit, cuts=(), kind=jnp.bfloat16):
    level = levels(stream_key, extent, cuts, -0.22, 0.18) if cuts else 1.0
    values = jax.random.normal(stream_key, extent, jnp.float32) * spread * level
    return jnp.minimum(jnp.maximum(values, -limit), limit).astype(kind)


def setup_inputs(seed: int = 0) -> dict:
    key_of = jax.random.split(jax.random.key(seed), 13)
    tokens = bell_draw(key_of[0], (SEQS, SEQ_LEN, D), 1.0, 6.0, ((0, 8), (1, 4)))
    cotangent = bell_draw(key_of[1], (SEQS, SEQ_LEN, D), 1.0, 6.0, ((0, 8), (1, 4)))
    lengths = draw_lengths(jax.random.fold_in(key_of[12], 71), 0)
    query_weight = bell_draw(key_of[3], (D, HEADS * HD), D ** -0.5, 0.125, ((0, 32),))
    key_weight = bell_draw(key_of[4], (D, KV * HD), D ** -0.5, 0.125, ((0, 32),))
    value_weight = bell_draw(key_of[5], (D, KV * HD), D ** -0.5, 0.125, ((0, 32),))
    output_weight = bell_draw(key_of[6], (HEADS * HD, D), (HEADS * HD // 64) ** -0.5, 1.0, ((0, 32),))
    gate_weight = bell_draw(key_of[7], (D, FF), D ** -0.5, 0.125, ((0, 8), (1, 4)))
    up_weight = bell_draw(key_of[8], (D, FF), D ** -0.5, 0.125, ((0, 8), (1, 4)))
    down_weight = bell_draw(key_of[9], (FF, D), FF ** -0.5, 0.078125, ((0, 4), (1, 8)))
    attention_gain = jnp.clip(1.0 + 0.1 * jax.random.normal(key_of[10], (D,), jnp.float32), 0.5, 1.5).astype(jnp.bfloat16)
    feed_gain = jnp.clip(1.0 + 0.1 * jax.random.normal(key_of[11], (D,), jnp.float32), 0.5, 1.5).astype(jnp.bfloat16)
    return {"tokens": tokens, "cotangent": cotangent, "lengths": lengths, "query_weight": query_weight, "key_weight": key_weight, "value_weight": value_weight, "output_weight": output_weight, "gate_weight": gate_weight, "up_weight": up_weight, "down_weight": down_weight, "attention_gain": attention_gain, "feed_gain": feed_gain}


@jax.custom_vjp
def low(v):
    return lax.optimization_barrier(v.astype(jnp.bfloat16)).astype(jnp.float32)

@jax.custom_vjp
def low_back(v):
    return v

def low_keep(v):
    return (low(v), None)

def low_pass(kept, grad):
    return (grad,)

def back_keep(v):
    return (v, None)

def back_low(kept, grad):
    return (low(grad),)
low.defvjp(low_keep, low_pass)
low_back.defvjp(back_keep, back_low)
epsilon = 1e-05
highest = lax.Precision.HIGHEST

def rms_norm(values, gain):
    return values * lax.rsqrt(lax.optimization_barrier(jnp.mean(values * values, axis=-1, keepdims=True)) + epsilon) * gain

def rope_tables(positions, width):
    half_width = width // 2
    frequency = jnp.power(10000.0, -2.0 * jnp.arange(half_width).astype(jnp.float32) / width)
    angles = positions.astype(jnp.float32)[:, None] * frequency[None, :]
    return (jnp.concatenate([jnp.cos(angles), jnp.cos(angles)], -1), jnp.concatenate([jnp.sin(angles), jnp.sin(angles)], -1))

def rotate(values, cos_table, sin_table):
    half_width = values.shape[-1] // 2
    turned = jnp.concatenate([-values[..., half_width:], values[..., :half_width]], -1)
    return values * cos_table[:, None, :] + turned * sin_table[:, None, :]

def layer(resid, params, length):
    query_weight, key_weight, value_weight, output_weight, gate_weight, up_weight, down_weight, attention_gain, feed_gain = params
    positions = jnp.arange(SEQ_LEN)
    cos_table, sin_table = rope_tables(positions, HD)
    valid_rows = (positions < length)[:, None]
    normed_one = low(rms_norm(resid, attention_gain))
    queries = low_back(jnp.dot(normed_one, query_weight, precision=highest)).reshape(SEQ_LEN, HEADS, HD)
    keys = low_back(jnp.dot(normed_one, key_weight, precision=highest)).reshape(SEQ_LEN, KV, HD)
    values = low_back(jnp.dot(normed_one, value_weight, precision=highest)).reshape(SEQ_LEN, KV, HD)
    group = HEADS // KV
    queries = low_back(low(rotate(queries, cos_table, sin_table)))
    keys = low_back(low(jnp.repeat(rotate(keys, cos_table, sin_table), group, axis=1)))
    values = low_back(low(jnp.repeat(values, group, axis=1)))

    def attend(triple):
        head_query, head_key, head_value = triple
        row_pos = jnp.arange(SEQ_LEN)
        allowed = (row_pos[None, :] <= row_pos[:, None]) & (row_pos[None, :] < length)
        scores = low_back(jnp.dot(head_query, head_key.T, precision=highest) * HD ** (-0.5))
        soft_probs = low(jax.nn.softmax(jnp.where(allowed, scores, -1e+30), axis=-1))
        return jnp.dot(soft_probs, head_value, precision=highest)
    per_head = lax.map(jax.checkpoint(attend), (queries.transpose(1, 0, 2), keys.transpose(1, 0, 2), values.transpose(1, 0, 2)))
    attended = low_back(low(per_head.transpose(1, 0, 2).reshape(SEQ_LEN, HEADS * HD)))
    branch = low_back(jnp.dot(attended, output_weight, precision=highest))
    middle = resid + branch
    normed_two = low(rms_norm(middle, feed_gain))
    gate_out = low_back(jnp.dot(normed_two, gate_weight, precision=highest))
    up_out = low_back(jnp.dot(normed_two, up_weight, precision=highest))
    hidden = low(jax.nn.silu(gate_out) * up_out)
    mixed = low_back(jnp.dot(hidden, down_weight, precision=highest))
    result = (middle + mixed) * valid_rows
    count_cells = length.astype(jnp.float32) * D
    norms = jnp.stack([jnp.sqrt(jnp.sum(jnp.where(valid_rows, member * member, 0.0)) / count_cells) for member in (resid, branch, mixed)])
    return (result, norms)

def reference(tokens, cotangent, lengths, query_weight, key_weight, value_weight, output_weight, gate_weight, up_weight, down_weight, attention_gain, feed_gain):
    weights = tuple((member.astype(jnp.float32) for member in (query_weight, key_weight, value_weight, output_weight, gate_weight, up_weight, down_weight, attention_gain, feed_gain)))

    def one_sequence(totals, packed):
        rows_in, grad_in, length = packed

        def forward(resid, params):
            return layer(resid, params, length)
        result, pull, norms = jax.vjp(forward, rows_in.astype(jnp.float32), weights, has_aux=True)
        input_grad, weight_grads = pull(grad_in.astype(jnp.float32))
        totals = jax.tree.map(jnp.add, totals, weight_grads)
        return (totals, (result.astype(jnp.bfloat16), input_grad.astype(jnp.bfloat16), norms))
    zeros = jax.tree.map(jnp.zeros_like, weights)
    totals, (block_out, input_grad, norms) = lax.scan(one_sequence, zeros, (tokens, cotangent, lengths))
    return (block_out, input_grad, totals[0], totals[1], totals[2], totals[3], totals[4], totals[5], totals[6], totals[7], totals[8], norms.T)
```

```python
import functools

import jax
import jax.numpy as jnp
from jax import lax
from jax.experimental import pallas as pl
from jax.experimental.pallas import tpu as pltpu
from jax.experimental.layout import Layout, with_layout_constraint
from jax.sharding import PartitionSpec as P

HEADS = 32
KV = 4
HD = 64
HALF = HD // 2
EPS = 1e-05
F32 = jnp.float32
BF16 = jnp.bfloat16
SCALE = HD ** (-0.5)
NEG = -1e30


def dot(left, right, left_dim, right_dim):
    return lax.dot_general(
        left, right, (((left_dim,), (right_dim,)), ((), ())), preferred_element_type=F32
    )


def swap(values, bit, count, axis="sp"):
    return lax.ppermute(values, axis, [(i, i ^ bit) for i in range(count)])


def order_of(count):
    order = [0]
    bit = count // 2
    while bit:
        order += [member ^ bit for member in order]
        bit //= 2
    return order


def spread(block, count, axis="sp", stop=1):
    parts = list(block) if isinstance(block, (list, tuple)) else [block]
    bit = count // (2 * len(parts))
    while bit >= stop:
        parts += [swap(part, bit, count, axis) for part in parts]
        bit //= 2
    return parts


def after(values, *others):
    return lax.optimization_barrier((values,) + others)[0]


def gather_rows(block, count):
    return jnp.concatenate(spread(block, count), axis=0)


def gather_bits(stack, count, high, low):
    me = lax.axis_index("dp")
    bit = high
    while bit >= low:
        got = swap(stack, bit, count, "dp")
        stack = widen(stack, got, (me & bit) != 0)
        bit //= 2
    return stack, got


def widen(mine, other, odd):
    first = jnp.where(odd, other, mine)
    second = jnp.where(odd, mine, other)
    return jnp.stack([first, second], axis=1).reshape((-1,) + mine.shape[1:])


def halve(left, bit, count, axis="dp"):
    side = (lax.axis_index(axis) & bit) // bit
    pairs = left.reshape((left.shape[0] // 2, 2) + left.shape[1:])
    leaving = lax.dynamic_index_in_dim(pairs, 1 - side, 1, False)
    staying = lax.dynamic_index_in_dim(pairs, side, 1, False)
    return staying, swap(leaving, bit, count, axis)


def join(staying, got):
    return staying.astype(F32) + got.astype(F32)


def finish(left, bit, count, axis="dp"):
    kind = left.dtype
    while bit < count:
        left = join(*halve(left.astype(kind), bit, count, axis))
        bit *= 2
    return left[0].astype(F32)


def blocks_of(values, count):
    return values.reshape((count, values.shape[0] // count) + values.shape[1:])


def reduce_near(product, rows, count):
    half = rows // 2
    got = swap(product(half, rows).astype(BF16), 1, count)
    return product(0, half) + got.astype(F32)


def reduce_pair(keep, send, count):
    return keep.astype(F32) + swap(send, 1, count).astype(F32)


def reduce_far(left, count):
    bit = 2
    while bit < count:
        half = left.shape[0] // 2
        got = swap(left[half:].astype(BF16), bit, count)
        left = left[:half] + got.astype(F32)
        bit *= 2
    return left


def flip_blocks(values, count, to_absolute):
    me = lax.axis_index("sp")
    order = order_of(count)
    size = values.shape[-1] // count
    blocks = [values[..., j * size : (j + 1) * size] for j in range(count)]
    if to_absolute:
        blocks = [blocks[order.index(offset)] for offset in range(count)]
    bit = 1
    while bit < count:
        odd = (me & bit) != 0
        blocks = [jnp.where(odd, blocks[j ^ bit], blocks[j]) for j in range(count)]
        bit *= 2
    if not to_absolute:
        blocks = [blocks[offset] for offset in order]
    return jnp.concatenate(blocks, axis=-1)


def row_major(values):
    return with_layout_constraint(values, Layout(major_to_minor=tuple(range(values.ndim))))


def block_of(length):
    for size in (256, 128):
        if length % size == 0:
            return size
    return length


def forward_kernel(block, len_ref, q_ref, k_ref, v_ref, out_ref, lse_ref):
    full = q_ref.shape[-1]
    length = len_ref[0]
    key_at = lax.broadcasted_iota(jnp.int32, (block, block), 0)
    row_at = lax.broadcasted_iota(jnp.int32, (block, block), 1)
    for step in range(full // block):
        start = step * block
        here = slice(start, start + block)
        queries = q_ref[0, :, here]
        near = jnp.dot(k_ref[here, :], queries, preferred_element_type=F32)
        near = jnp.where((key_at <= row_at) & (key_at + start < length), near, NEG)
        top = jnp.max(near, axis=0, keepdims=True)
        if start:
            far = jnp.dot(k_ref[0:start, :], queries, preferred_element_type=F32)
            top = jnp.maximum(top, jnp.max(far, axis=0, keepdims=True))
        near = jnp.exp(near - top)
        total = jnp.sum(near, axis=0, keepdims=True)
        result = jnp.dot(v_ref[:, here], near.astype(BF16), preferred_element_type=F32)
        if start:
            far = jnp.exp(far - top)
            total = total + jnp.sum(far, axis=0, keepdims=True)
            result = result + jnp.dot(
                v_ref[:, 0:start], far.astype(BF16), preferred_element_type=F32
            )
        out_ref[0, :, here] = (result / total).astype(BF16)
        lse_ref[0, :, here] = top + jnp.log(total)


def attend_forward(queries, keys, values_t, length):
    heads, _, full = queries.shape
    block = block_of(full)
    return pl.pallas_call(
        functools.partial(forward_kernel, block),
        grid=(heads,),
        in_specs=[
            pl.BlockSpec(memory_space=pltpu.SMEM),
            pl.BlockSpec((1, HD, full), lambda h: (h, 0, 0)),
            pl.BlockSpec((full, HD), lambda h: (0, 0)),
            pl.BlockSpec((HD, full), lambda h: (0, 0)),
        ],
        out_specs=[
            pl.BlockSpec((1, HD, full), lambda h: (h, 0, 0)),
            pl.BlockSpec((1, 1, full), lambda h: (h, 0, 0)),
        ],
        out_shape=[
            jax.ShapeDtypeStruct((heads, HD, full), BF16),
            jax.ShapeDtypeStruct((heads, 1, full), F32),
        ],
        compiler_params=pltpu.CompilerParams(vmem_limit_bytes=48 * 2**20),
        cost_estimate=pl.CostEstimate(
            flops=2 * heads * full * full * HD,
            bytes_accessed=heads * full * HD * 4,
            transcendentals=heads * full,
        ),
    )(length, queries, keys, values_t)


def backward_kernel(
    block, len_ref, q_ref, grad_ref, k_ref, kt_ref, v_ref, lse_ref, delta_ref, gq_ref, gk_ref, gv_ref, acc_ref
):
    full = q_ref.shape[-1]
    length = len_ref[0]

    @pl.when(pl.program_id(0) == 0)
    def _():
        gk_ref[...] = jnp.zeros_like(gk_ref)
        gv_ref[...] = jnp.zeros_like(gv_ref)

    key_at = lax.broadcasted_iota(jnp.int32, (block, block), 0)
    row_at = lax.broadcasted_iota(jnp.int32, (block, block), 1)
    for step in range(full // block):
        start = step * block
        here = slice(start, start + block)
        pieces = [(start, start + block, True)]
        if start + block < full:
            pieces.append((start + block, full, False))
        for low, high, edge in pieces:
            rows = slice(low, high)
            queries = q_ref[0, :, rows]
            grads = grad_ref[0, :, rows]
            scores = jnp.dot(k_ref[here, :], queries, preferred_element_type=F32)
            probs = jnp.exp(scores - lse_ref[0, :, rows])
            if edge:
                probs = jnp.where((key_at <= row_at) & (key_at + start < length), probs, 0.0)
            prob_grad = jnp.dot(v_ref[here, :], grads, preferred_element_type=F32)
            score_grad = (probs * (prob_grad - delta_ref[0, :, rows])).astype(BF16)
            gk_ref[here, :] += dot(score_grad, queries, 1, 1)
            gv_ref[here, :] += dot(probs.astype(BF16), grads, 1, 1)
            part = jnp.dot(kt_ref[:, here], score_grad, preferred_element_type=F32)
            if step == 0:
                acc_ref[:, rows] = part
            else:
                acc_ref[:, rows] += part
    gq_ref[0] = (acc_ref[...] * SCALE).astype(BF16)


def attend_backward(queries, grads, keys, keys_t, values, lse, delta, length):
    heads, _, full = queries.shape
    block = block_of(full)
    per_head = pl.BlockSpec((1, HD, full), lambda h: (h, 0, 0))
    per_row = pl.BlockSpec((1, 1, full), lambda h: (h, 0, 0))
    whole = pl.BlockSpec((full, HD), lambda h: (0, 0))
    return pl.pallas_call(
        functools.partial(backward_kernel, block),
        grid=(heads,),
        in_specs=[
            pl.BlockSpec(memory_space=pltpu.SMEM),
            per_head,
            per_head,
            whole,
            pl.BlockSpec((HD, full), lambda h: (0, 0)),
            whole,
            per_row,
            per_row,
        ],
        out_specs=[per_head, whole, whole],
        out_shape=[
            jax.ShapeDtypeStruct((heads, HD, full), BF16),
            jax.ShapeDtypeStruct((full, HD), F32),
            jax.ShapeDtypeStruct((full, HD), F32),
        ],
        scratch_shapes=[pltpu.VMEM((HD, full), F32)],
        compiler_params=pltpu.CompilerParams(vmem_limit_bytes=48 * 2**20),
        cost_estimate=pl.CostEstimate(
            flops=4 * heads * full * full * HD,
            bytes_accessed=heads * full * HD * 6,
            transcendentals=heads * full,
        ),
    )(length, queries, grads, keys, keys_t, values, lse, delta)


TILE = 256


def tiles_of(hidden):
    if hidden % 128:
        return [(0, hidden)]
    return [(low, min(low + TILE, hidden)) for low in range(0, hidden, TILE)]


def interleave(gate, up):
    return jnp.concatenate(
        [array[:, low:high] for low, high in tiles_of(gate.shape[1]) for array in (gate, up)], axis=1
    )


def separate(both):
    pieces = tiles_of(both.shape[1] // 2)
    gate = [both[:, 2 * low : low + high] for low, high in pieces]
    up = [both[:, low + high : 2 * high] for low, high in pieces]
    return jnp.concatenate(gate, axis=1), jnp.concatenate(up, axis=1)


def activate(gate, up, grad):
    sig = 1.0 / (1.0 + jnp.exp(-gate))
    act = gate * sig
    slope = sig * (1.0 + gate * (1.0 - sig))
    return (act * up).astype(BF16), (grad * up * slope).astype(BF16), (grad * act).astype(BF16)


def feed_kernel(last, blocks, *refs):
    n2_parts, grad_parts = refs[:blocks], refs[blocks : 2 * blocks]
    refs = refs[2 * blocks :]
    gu_ref, down_ref, hid_ref, out_ref, n2_out, grad_out = refs[:6]
    refs = refs[6:]
    n2_ref, grad_ref, in_sems, out_sems = refs
    part = n2_parts[0].shape[0]
    step = pl.program_id(0)
    count = pl.num_programs(0)

    def arriving(j):
        here = pl.ds(j * part, part)
        return (
            pltpu.make_async_copy(n2_parts[j], n2_ref.at[here], in_sems.at[2 * j]),
            pltpu.make_async_copy(grad_parts[j], grad_ref.at[here], in_sems.at[2 * j + 1]),
        )

    def leaving():
        return (
            pltpu.make_async_copy(n2_ref, n2_out, out_sems.at[0]),
            pltpu.make_async_copy(grad_ref, grad_out, out_sems.at[1]),
        )

    def run(size, first):
        if first:
            for j in range(blocks):
                for copy in arriving(j):
                    copy.start()
        for j in range(blocks):
            here = slice(j * part, (j + 1) * part)
            if first:
                for copy in arriving(j):
                    copy.wait()
            values = n2_ref[here, :]
            if size == TILE:
                gate = jnp.dot(values, gu_ref[:, :size], preferred_element_type=F32)
                up = jnp.dot(values, gu_ref[:, size : 2 * size], preferred_element_type=F32)
            else:
                both = jnp.dot(values, gu_ref[:, : 2 * size], preferred_element_type=F32)
                gate, up = both[:, :size], both[:, size:]
            grad = jnp.dot(grad_ref[here, :], down_ref[:, :size], preferred_element_type=F32)
            hid, gate_grad, up_grad = activate(gate, up, grad)
            hid_ref[here, :size] = hid
            out_ref[here, :size] = gate_grad
            out_ref[here, size : 2 * size] = up_grad
        if first:
            for copy in leaving():
                copy.start()

    @pl.when(step == 0)
    def _():
        run(TILE, True)

    @pl.when((step > 0) & (step < count - 1))
    def _():
        run(TILE, False)

    @pl.when(step == count - 1)
    def _():
        run(last, False)
        for copy in leaving():
            copy.wait()


def feed(n2_parts, grad_parts, gu_w, down_t):
    blocks = len(n2_parts)
    part, width = n2_parts[0].shape
    rows = blocks * part
    hidden = down_t.shape[1]
    pieces = tiles_of(hidden)
    if hidden % 128 or len(pieces) < 3:
        n2 = jnp.concatenate(n2_parts, axis=0)
        grad = jnp.concatenate(grad_parts, axis=0)
        gate_w, up_w = separate(gu_w)
        hid, gate_grad, up_grad = activate(
            dot(n2, gate_w, 1, 0), dot(n2, up_w, 1, 0), dot(grad, down_t, 1, 0)
        )
        return hid, interleave(gate_grad, up_grad), n2, grad
    last = pieces[-1][1] - pieces[-1][0]
    hbm = pl.BlockSpec(memory_space=pl.ANY)
    return pl.pallas_call(
        functools.partial(feed_kernel, last, blocks),
        grid=(len(pieces),),
        in_specs=[hbm] * (2 * blocks)
        + [
            pl.BlockSpec((width, 2 * TILE), lambda j: (0, j)),
            pl.BlockSpec((width, TILE), lambda j: (0, j)),
        ],
        out_specs=[
            pl.BlockSpec((rows, TILE), lambda j: (0, j)),
            pl.BlockSpec((rows, 2 * TILE), lambda j: (0, j)),
            hbm,
            hbm,
        ],
        out_shape=[
            jax.ShapeDtypeStruct((rows, hidden), BF16),
            jax.ShapeDtypeStruct((rows, 2 * hidden), BF16),
            jax.ShapeDtypeStruct((rows, width), BF16),
            jax.ShapeDtypeStruct((rows, width), BF16),
        ],
        scratch_shapes=[
            pltpu.VMEM((rows, width), BF16),
            pltpu.VMEM((rows, width), BF16),
            pltpu.SemaphoreType.DMA((2 * blocks,)),
            pltpu.SemaphoreType.DMA((2,)),
        ],
        compiler_params=pltpu.CompilerParams(vmem_limit_bytes=56 * 2**20),
        cost_estimate=pl.CostEstimate(
            flops=rows * width * hidden,
            bytes_accessed=4 * rows * width,
            transcendentals=rows,
        ),
    )(*n2_parts, *grad_parts, gu_w, down_t)


def rotate(values, cos, sin):
    one, two = values[:, :HALF], values[:, HALF:]
    return jnp.concatenate([one * cos - two * sin, two * cos + one * sin], axis=1)


def rotate_back(grad, cos, sin):
    one, two = grad[:, :HALF], grad[:, HALF:]
    return jnp.concatenate([one * cos + two * sin, two * cos - one * sin], axis=1)


def fits(part):
    return part % 128 == 0


def place(at_ref, j, part):
    return pl.ds(pl.multiple_of(at_ref[j] * part, 128), part)


SMALL = pl.CostEstimate(flops=1000000, bytes_accessed=1000000, transcendentals=1000)
PARAMS = pltpu.CompilerParams(vmem_limit_bytes=56 * 2**20)
IN_HBM = pl.BlockSpec(memory_space=pl.ANY)
IN_VMEM = pl.BlockSpec(memory_space=pltpu.VMEM)
IN_SMEM = pl.BlockSpec(memory_space=pltpu.SMEM)


def fetch(parts, buf_ref, sems):
    part = parts[0].shape[0]
    return [
        pltpu.make_async_copy(source, buf_ref.at[pl.ds(j * part, part)], sems.at[j])
        for j, source in enumerate(parts)
    ]


def project_kernel(blocks, at_ref, *refs):
    parts = refs[:blocks]
    gain_ref, w_ref, cos_ref, sin_ref = refs[blocks : blocks + 4]
    n1_out, q_ref, kt_ref, vt_ref, k_ref, v_ref, buf_ref, in_sems, out_sems = refs[blocks + 4 :]
    part = parts[0].shape[0]
    heads = q_ref.shape[0]
    coming = fetch(parts, buf_ref, in_sems)
    for copy in coming:
        copy.start()
    leaving = []
    for j in range(blocks):
        coming[j].wait()
        for low in range(j * part, (j + 1) * part, 128):
            here = slice(low, low + 128)
            values = buf_ref[here, :].astype(F32)
            scale = lax.rsqrt(jnp.mean(values * values, axis=-1, keepdims=True) + EPS)
            buf_ref[here, :] = (values * scale * gain_ref[...]).astype(BF16)
        rows = pl.ds(j * part, part)
        leaving.append(pltpu.make_async_copy(buf_ref.at[rows], n1_out.at[rows], out_sems.at[j]))
        leaving[-1].start()
        proj = dot(w_ref[...], buf_ref[j * part : (j + 1) * part, :], 1, 1)
        cos = cos_ref[:, j * part : (j + 1) * part][None]
        sin = sin_ref[:, j * part : (j + 1) * part][None]
        there = place(at_ref, j, part)
        cut = heads * HD
        q = rotate(proj[:cut].reshape(heads, HD, part), cos, sin) * SCALE
        q_ref[:, :, there] = q.astype(BF16)
        k = rotate(proj[cut : cut + HD].reshape(1, HD, part), cos, sin)[0]
        v = proj[cut + HD :]
        kt_ref[:, there] = k.astype(BF16)
        vt_ref[:, there] = v.astype(BF16)
        k_ref[there, :] = k.T.astype(BF16)
        v_ref[there, :] = v.T.astype(BF16)
    for copy in leaving:
        copy.wait()


def project(parts, at, gain, w_t, cos, sin, heads):
    blocks = len(parts)
    part, width = parts[0].shape
    full = blocks * part
    if not fits(part):
        cut = heads * HD
        values = jnp.concatenate(parts, axis=0).astype(F32)
        scale = lax.rsqrt(jnp.mean(values * values, axis=-1, keepdims=True) + EPS)
        n1 = (values * scale * gain).astype(BF16)
        proj = dot(w_t, n1, 1, 1)
        q = rotate(proj[:cut].reshape(heads, HD, full), cos[None], sin[None]) * SCALE
        k = rotate(proj[cut : cut + HD].reshape(1, HD, full), cos[None], sin[None])
        both = jnp.concatenate([q.reshape(cut, full), k[0], proj[cut + HD :]], axis=0).astype(BF16)
        both = flip_blocks(both, blocks, True)
        k_t, v_t = both[cut : cut + HD], both[cut + HD :]
        return n1, both[:cut].reshape(heads, HD, full), k_t, v_t, k_t.T, v_t.T
    flat = jax.ShapeDtypeStruct((HD, full), BF16)
    tall = jax.ShapeDtypeStruct((full, HD), BF16)
    return pl.pallas_call(
        functools.partial(project_kernel, blocks),
        in_specs=[IN_SMEM] + [IN_HBM] * blocks + [IN_VMEM] * 4,
        out_specs=[IN_HBM] + [IN_VMEM] * 5,
        out_shape=[
            jax.ShapeDtypeStruct((full, width), BF16),
            jax.ShapeDtypeStruct((heads, HD, full), BF16),
            flat,
            flat,
            tall,
            tall,
        ],
        scratch_shapes=[
            pltpu.VMEM((full, width), BF16),
            pltpu.SemaphoreType.DMA((blocks,)),
            pltpu.SemaphoreType.DMA((blocks,)),
        ],
        compiler_params=PARAMS,
        cost_estimate=SMALL,
    )(at, *parts, gain, w_t, cos, sin)


def merge_kernel(blocks, at_ref, att_ref, w_ref, keep_ref, send_ref):
    part = att_ref.shape[1] // blocks
    for j in range(blocks):
        mine = att_ref[:, place(at_ref, j, part)]
        product = dot(mine, w_ref[...], 0, 0).astype(BF16)
        target, slot = (keep_ref, j) if j < blocks // 2 else (send_ref, j - blocks // 2)
        target[slot * part : (slot + 1) * part, :] = product


def merge_heads(att, at, out_w, blocks):
    cut, full = att.shape
    half = full // 2
    width = out_w.shape[1]
    if not fits(full // blocks):
        product = dot(flip_blocks(att, blocks, False), out_w, 0, 0).astype(BF16)
        return product[:half], product[half:]
    return pl.pallas_call(
        functools.partial(merge_kernel, blocks),
        in_specs=[IN_SMEM, IN_VMEM, IN_VMEM],
        out_specs=[IN_VMEM, IN_VMEM],
        out_shape=[jax.ShapeDtypeStruct((half, width), BF16)] * 2,
        compiler_params=PARAMS,
        cost_estimate=SMALL,
    )(at, att, out_w)


def split_kernel(blocks, has_sum, at_ref, *refs):
    parts = refs[:blocks]
    w_ref, att_ref = refs[blocks : blocks + 2]
    refs = refs[blocks + 2 :]
    if has_sum:
        sum_ref, refs = refs[0], refs[1:]
    grad_ref, delta_ref, wgrad_ref, buf_ref, acc_ref, sems = refs
    part = parts[0].shape[0]
    heads = att_ref.shape[0]
    coming = fetch(parts, buf_ref, sems)
    for copy in coming:
        copy.start()
    for j in range(blocks):
        coming[j].wait()
        rows = buf_ref[j * part : (j + 1) * part, :]
        there = place(at_ref, j, part)
        att = att_ref[:, :, there]
        grad = dot(w_ref[...], rows, 1, 1).astype(BF16).reshape(heads, HD, part)
        grad_ref[:, :, there] = grad
        delta_ref[:, :, there] = jnp.sum(
            grad.astype(F32) * att.astype(F32), axis=1, keepdims=True
        )
        share = jnp.dot(att.reshape(heads * HD, part), rows, preferred_element_type=F32)
        if j:
            acc_ref[...] += share
        elif has_sum:
            acc_ref[...] = sum_ref[...] + share
        else:
            acc_ref[...] = share
    wgrad_ref[...] = acc_ref[...].astype(wgrad_ref.dtype)


def split_heads(parts, at, out_w, att, so_far):
    blocks = len(parts)
    part, width = parts[0].shape
    heads, _, full = att.shape
    kind = F32 if so_far is None else BF16
    if not fits(part):
        rows = jnp.concatenate(parts, axis=0)
        grad = flip_blocks(dot(out_w, rows, 1, 1).astype(BF16), blocks, True)
        grad = grad.reshape(heads, HD, full)
        delta = jnp.sum(grad.astype(F32) * att.astype(F32), axis=1, keepdims=True)
        wgrad = dot(flip_blocks(att.reshape(heads * HD, full), blocks, False), rows, 1, 0)
        return grad, delta, (wgrad if so_far is None else so_far + wgrad).astype(kind)
    more = [] if so_far is None else [so_far]
    return pl.pallas_call(
        functools.partial(split_kernel, blocks, bool(more)),
        in_specs=[IN_SMEM] + [IN_HBM] * blocks + [IN_VMEM] * (2 + len(more)),
        out_specs=[IN_VMEM] * 3,
        out_shape=[
            jax.ShapeDtypeStruct((heads, HD, full), BF16),
            jax.ShapeDtypeStruct((heads, 1, full), F32),
            jax.ShapeDtypeStruct((heads * HD, width), kind),
        ],
        scratch_shapes=[
            pltpu.VMEM((full, width), BF16),
            pltpu.VMEM((heads * HD, width), F32),
            pltpu.SemaphoreType.DMA((blocks,)),
        ],
        compiler_params=PARAMS,
        cost_estimate=SMALL,
    )(at, *parts, out_w, att, *more)


def return_kernel(blocks, has_sum, at_ref, *refs):
    gq_ref, gk_ref, gv_ref, cos_ref, sin_ref, w_ref, n1_in = refs[:7]
    refs = refs[7:]
    if has_sum:
        sum_ref, refs = refs[0], refs[1:]
    keep_ref, send_ref, wgrad_ref, buf_ref, acc_ref, sems = refs
    heads, _, full = gq_ref.shape
    part = full // blocks
    coming = fetch([n1_in.at[pl.ds(j * part, part)] for j in range(blocks)], buf_ref, sems)
    for copy in coming:
        copy.start()
    for j in range(blocks):
        there = place(at_ref, j, part)
        cos = cos_ref[:, j * part : (j + 1) * part][None]
        sin = sin_ref[:, j * part : (j + 1) * part][None]
        gq = rotate_back(gq_ref[:, :, there].astype(F32), cos, sin)
        gk = rotate_back(gk_ref[there, :].T[None], cos, sin)[0]
        grad = jnp.concatenate(
            [
                gq.reshape(heads * HD, part).astype(BF16),
                gk.astype(BF16),
                gv_ref[there, :].T.astype(BF16),
            ],
            axis=0,
        )
        product = dot(grad, w_ref[...], 0, 0).astype(BF16)
        target, slot = (keep_ref, j) if j < blocks // 2 else (send_ref, j - blocks // 2)
        target[slot * part : (slot + 1) * part, :] = product
        coming[j].wait()
        share = jnp.dot(grad, buf_ref[j * part : (j + 1) * part, :], preferred_element_type=F32)
        if j:
            acc_ref[...] += share
        elif has_sum:
            acc_ref[...] = sum_ref[...] + share
        else:
            acc_ref[...] = share
    if has_sum:
        groups, _, columns = wgrad_ref.shape
        for d in range(groups):
            wgrad_ref[d] = acc_ref[:, d * columns : (d + 1) * columns].astype(BF16)
    else:
        wgrad_ref[...] = acc_ref[...]


def return_rows(gq, gk, gv, at, cos, sin, w_t, n1, so_far, groups):
    heads, _, full = gq.shape
    blocks = at.shape[0]
    columns, width = w_t.shape
    half = full // 2
    last = so_far is not None
    if not fits(full // blocks):
        back = jnp.concatenate([gq.reshape(heads * HD, full).astype(F32), gk.T, gv.T], axis=0)
        back = flip_blocks(back, blocks, False)
        turned = rotate_back(
            back[: heads * HD + HD].reshape(heads + 1, HD, full), cos[None], sin[None]
        )
        grad = jnp.concatenate(
            [turned.reshape(heads * HD + HD, full), back[heads * HD + HD :]], axis=0
        ).astype(BF16)
        product = dot(grad, w_t, 0, 0).astype(BF16)
        wgrad = dot(grad, n1, 1, 0)
        if last:
            wgrad = (so_far + wgrad).astype(BF16)
            wgrad = wgrad.reshape(columns, groups, width // groups).transpose(1, 0, 2)
        return product[:half], product[half:], wgrad
    more = [so_far] if last else []
    shape = (groups, columns, width // groups) if last else (columns, width)
    return pl.pallas_call(
        functools.partial(return_kernel, blocks, last),
        in_specs=[IN_SMEM] + [IN_VMEM] * 6 + [IN_HBM] + [IN_VMEM] * len(more),
        out_specs=[IN_VMEM] * 3,
        out_shape=[
            jax.ShapeDtypeStruct((half, width), BF16),
            jax.ShapeDtypeStruct((half, width), BF16),
            jax.ShapeDtypeStruct(shape, BF16 if last else F32),
        ],
        scratch_shapes=[
            pltpu.VMEM((full, width), BF16),
            pltpu.VMEM((columns, width), F32),
            pltpu.SemaphoreType.DMA((blocks,)),
        ],
        compiler_params=PARAMS,
        cost_estimate=SMALL,
    )(at, gq, gk, gv, cos, sin, w_t, n1, *more)


def body(
    tokens,
    cotangent,
    lengths,
    query_weight,
    key_weight,
    value_weight,
    output_weight,
    gate_weight,
    up_weight,
    down_weight,
    attention_gain,
    feed_gain,
):
    seqs, local, width = tokens.shape
    sp = lax.axis_size("sp")
    dp = lax.axis_size("dp")
    me = lax.axis_index("sp")
    full = local * sp
    heads = HEADS // sp
    own_rows = query_weight.shape[0]
    dp_rows = own_rows * sp
    q_cols = heads * HD
    order = order_of(sp)
    hidden = gate_weight.shape[1]

    positions = me * local + jnp.arange(local)
    valid = positions[None, :] < lengths[:, None]

    def pick(array, target):
        head = target * KV // sp
        return array[:, head * HD : (head + 1) * HD]

    extra = jnp.concatenate(
        [attention_gain[:, None], feed_gain[:, None], jnp.zeros((own_rows, 126), BF16)], axis=1
    )
    to_send = jnp.stack(
        [
            jnp.concatenate(
                [
                    query_weight[:, t * q_cols : (t + 1) * q_cols],
                    pick(key_weight, t),
                    pick(value_weight, t),
                    extra,
                ],
                axis=1,
            )
            for t in range(sp)
        ]
    )
    proj_cols = q_cols + 2 * HD
    in_block = lax.all_to_all(to_send, "sp", 0, 0, tiled=True).reshape(dp_rows, proj_cols + 128)
    total = dp * sp
    there = [(n, (n % dp) * sp + n // dp) for n in range(total)]
    back = [(b, a) for a, b in there]
    out_block = lax.ppermute(output_weight, ("dp", "sp"), there)
    out_cols = own_rows * width // dp_rows
    attn_mine = jnp.concatenate([in_block, out_block.reshape(dp_rows, out_cols)], axis=1)
    attn_all = row_major(lax.all_gather(row_major(attn_mine), "dp", axis=0, tiled=True))
    there_is = jnp.isfinite(in_block[0, 0].astype(F32))

    def later(array):
        return jnp.where(there_is, array, jnp.zeros_like(array))

    half = dp // 2
    gu_mine = interleave(gate_weight, up_weight)
    gu_w = row_major(lax.all_gather(row_major(gu_mine), "dp", axis=0, tiled=True))
    held = later(tokens)
    cot_local = jnp.where(valid[..., None], cotangent, jnp.zeros_like(cotangent))
    rows_far, cot_far = [], []
    chain = []
    for source, far in ((held, rows_far), (cot_local, cot_far)):
        for s in range(seqs):
            far.append(spread(after(source[s], *chain), sp, "sp", 2))
            chain = far[-1][1:]
    rows_all = [spread(far, sp) for far in rows_far]
    cot_parts = [spread(far, sp) for far in cot_far]
    down_a, _ = gather_bits(after(down_weight.T, attn_all)[None], dp, half, half)
    down_b, down_far = gather_bits(down_a, dp, half // 2, 2)
    down_c, down_near = gather_bits(down_b, dp, 1, 1)
    proj_t = attn_all[:, :proj_cols].T
    gains = attn_all[:, proj_cols : proj_cols + 2].astype(F32)
    gain_one, gain_two = gains[:, 0], gains[:, 1]
    out_w = attn_all[:, proj_cols + 128 :].reshape(q_cols, width)
    down_t = down_c.reshape(width, hidden)
    rows_all[0][0] = after(rows_all[0][0], *rows_far[-1])
    early = [[part for far in cot_far for part in far], []]

    row_pos = jnp.concatenate([(me ^ member) * local + jnp.arange(local) for member in order])
    frequency = jnp.power(10000.0, -2.0 * jnp.arange(HALF).astype(F32) / HD)
    angles = frequency[:, None] * row_pos.astype(F32)[None, :]
    cos, sin = jnp.cos(angles), jnp.sin(angles)
    at = jnp.stack([me ^ member for member in order]).astype(jnp.int32)

    def norm(values, gain):
        scale = lax.rsqrt(jnp.mean(values * values, axis=-1, keepdims=True) + EPS)
        return values * scale * gain

    def norm_back(grad, values, gain):
        scale = lax.rsqrt(jnp.mean(values * values, axis=-1, keepdims=True) + EPS)
        scaled = grad * gain
        return scale * scaled - values * scale**3 * jnp.mean(scaled * values, axis=-1, keepdims=True)

    normed_one, saved, branches, middles, normed_two, n2_far = [], [], [], [], [], []
    for s in range(seqs):
        length = lengths[s : s + 1]
        parts = list(rows_all[s])
        if s:
            parts[0] = after(parts[0], begun)
        n1, q, k_t, v_t, k, v = project(parts, at, gain_one[None], proj_t, cos, sin, heads)
        normed_one.append(n1)
        q = after(q, *cot_parts[s], *early[min(s, 1)], *branches)
        att, lse = attend_forward(q, k, v_t, length)
        if s:
            normed_two.append(spread([after(part, att) for part in n2_far[-1]], sp))
        flat = att.reshape(q_cols, full)
        flat = after(flat, *normed_two[-1], gu_w, down_near) if s else after(flat, down_far)
        begun = reduce_pair(*merge_heads(flat, at, out_w, sp), sp)
        branch = reduce_far(begun, sp)
        middle = tokens[s].astype(F32) + branch
        n2_far.append(spread(norm(middle, gain_two).astype(BF16), sp, "sp", 2))
        saved.append((q, k, k_t, v, att, lse))
        branches.append(branch)
        middles.append(middle)

    def mlp_near(hid, keep):
        return reduce_near(
            lambda lo, hi: dot((hid if lo else keep)[lo:hi], down_t, 1, 1), full, sp
        )

    begun_mixed = []
    hiddens, gu_grads, n2_grads, middle_grads, grad_rows, cot_all = [], [], [], [], [], []
    down_wgrad = 0.0
    for s in range(seqs):
        n2 = [after(part, begun) for part in normed_two[s]]
        made = feed(n2, cot_parts[s], gu_w, down_t)
        hid, gu_grad, normed_two[s], cot_all_s = made
        cot_all.append(cot_all_s)
        hiddens.append(hid)
        gu_grads.append(gu_grad)
        if s < seqs - 1:
            low, high = n2_far[s + 1][0], n2_far[s + 1]
            hid = after(hid, low)
            down_wgrad = row_major(dot(cot_all[s], hid, 0, 0))
            begun_mixed.append(mlp_near(hid, hid))
            high = high + [down_wgrad, begun_mixed[0]]
        else:
            low, high = n2_grads[0], [n2_grads[0]]
        send, keep = after(gu_grad, low), after(gu_grad, *high)
        begun = reduce_near(
            lambda lo, hi: dot((keep if lo == 0 else send)[lo:hi], gu_w, 1, 1), full, sp
        )
        n2_grads.append(reduce_far(begun, sp))
        if s < seqs - 1:
            normed_two.append(spread(n2_far[s + 1], sp))
    gu_wgrad = 0.0
    for s in range(seqs):
        held = after(n2_grads[s], gu_grads[-1]) if s == 0 else after(n2_grads[s], gu_wgrad)
        middle_grads.append(cot_local[s].astype(F32) + norm_back(held, middles[s], gain_two))
        parts = spread(middle_grads[s].astype(BF16), sp, "sp", 2)
        far_rows = parts[1:]
        if s == 0:
            gu_wgrad = dot(after(normed_two[0], begun, middle_grads[0]), gu_grads[0], 0, 0)
            parts = [after(part, gu_wgrad) for part in parts]
        grad_rows.append(spread(parts, sp))
        if s == 0:
            for t in range(1, seqs):
                gu_wgrad = gu_wgrad + dot(after(normed_two[t], *grad_rows[0]), gu_grads[t], 0, 0)
            gu_wgrad = gu_wgrad.astype(BF16)
    rows = after(cot_all[-1], middle_grads[-1])
    down_wgrad = down_wgrad + dot(rows, hiddens[-1], 0, 0)
    down_wgrad = down_wgrad.astype(BF16)
    hid = after(hiddens[-1], down_wgrad)
    begun_mixed.append(mlp_near(hid, after(hid, *far_rows)))

    feed_wgrad = jnp.concatenate([gu_wgrad, down_wgrad], axis=1)
    feed_grad = row_major(
        lax.psum_scatter(row_major(feed_wgrad), "dp", scatter_dimension=0, tiled=True)
    )

    def norm_sums(mixed):
        sums = jnp.stack(
            [
                jnp.stack(
                    [
                        jnp.sum(jnp.where(valid[s][:, None], member[s] * member[s], 0.0))
                        for s in range(seqs)
                    ]
                )
                for member in ([tokens[s].astype(F32) for s in range(seqs)], branches, mixed)
            ]
        )
        bit = 1
        while bit < sp:
            sums = sums + swap(sums, bit, sp)
            bit *= 2
        return sums

    proj_wgrad = None
    out_wgrad = None
    input_grads = []
    for s in range(seqs):
        q, k, k_t, v, att, lse = saved[s]
        rows = list(grad_rows[s])
        rows[0] = after(rows[0], mark) if s else after(rows[0], *far_rows, *begun_mixed)
        att_grad, delta, out_wgrad = split_heads(rows, at, out_w, att, out_wgrad)
        if s:
            q = after(q, begun)
            staying, got = halve(blocks_of(out_wgrad, dp), 1, dp)
        gq, gk, gv = attend_backward(q, att_grad, k, k_t, v, lse, delta, lengths[s : s + 1])
        mark = gq
        if s == 0:
            mixed = [reduce_far(after(begun_mixed[0], att_grad), sp)]
            gq = after(gq, mixed[0])
            mixed += [reduce_far(after(begun_mixed[t], mark), sp) for t in range(1, seqs)]
        else:
            gq = after(gq, got, *mixed, n1_grad)
        keep, send, proj_wgrad = return_rows(
            gq, gk, gv, at, cos, sin, proj_t, normed_one[s], proj_wgrad, dp
        )
        begun = reduce_pair(keep, send, sp)
        if s == 0:
            n1_grad = reduce_far(begun, sp)
        else:
            out_grad = finish(join(staying, after(got, mark)).astype(BF16), 2, dp)
            sums = norm_sums(mixed)
            n1_grad = reduce_far(after(begun, sums), sp)
        rest = norm_back(n1_grad, tokens[s].astype(F32), gain_one)
        input_grads.append((middle_grads[s] + rest).astype(BF16))
    input_grad = jnp.stack(input_grads)
    feed_grad = after(feed_grad, n1_grad).astype(F32)
    gate_out, up_out = separate(feed_grad[:, : 2 * hidden])
    down_out = feed_grad[:, 2 * hidden :].T
    staying, got = halve(proj_wgrad, 1, dp)
    left = join(staying, after(got, begun)).astype(BF16)
    staying, got = halve(left, 2, dp)
    left = join(staying, after(got, n1_grad)).astype(BF16)
    proj_grad = finish(left, 4, dp)
    out_grad = lax.ppermute(out_grad.astype(BF16), ("dp", "sp"), back).astype(F32)

    block_out = jnp.stack(
        [((middles[s] + mixed[s]) * valid[s][:, None]).astype(BF16) for s in range(seqs)]
    )
    proj_grad = proj_grad.astype(BF16).reshape(proj_cols, sp, own_rows).transpose(1, 0, 2)
    proj_grad = lax.all_to_all(proj_grad, "sp", 0, 0, tiled=True).astype(F32)
    query_grad = proj_grad[:, :q_cols].transpose(2, 0, 1).reshape(own_rows, HEADS * HD)

    def kv_grad(array):
        copies = array.reshape(KV, sp // KV, HD, own_rows).sum(axis=1)
        return copies.transpose(2, 0, 1).reshape(own_rows, KV * HD)

    key_grad = kv_grad(proj_grad[:, q_cols : q_cols + HD])
    value_grad = kv_grad(proj_grad[:, q_cols + HD :])

    def rowwise(weight, grad):
        return jnp.sum(weight.astype(F32) * grad, axis=1)

    gain_one_grad = (
        rowwise(query_weight, query_grad)
        + rowwise(key_weight, key_grad)
        + rowwise(value_weight, value_grad)
    ) / attention_gain.astype(F32)
    shares = rowwise(gate_weight, gate_out) + rowwise(up_weight, up_out)
    gain_two_grad = finish(blocks_of(shares, sp), 1, sp, "sp") / feed_gain.astype(F32)

    branch_norms = jnp.sqrt(sums / (lengths.astype(F32) * width))
    return (
        block_out,
        input_grad,
        query_grad,
        key_grad,
        value_grad,
        out_grad,
        gate_out,
        up_out,
        down_out,
        gain_one_grad,
        gain_two_grad,
        branch_norms,
    )


def solution(mesh):
    rows = P(("dp", "sp"), None)
    gain = P(("dp", "sp"))
    seq = P("dp", "sp", None)
    in_specs = (
        seq, seq, P("dp"), rows, rows, rows, rows,
        P("dp", "sp"), P("dp", "sp"), P("sp", "dp"), gain, gain,
    )
    out_specs = (
        seq, seq, rows, rows, rows, rows,
        P("dp", "sp"), P("dp", "sp"), P("sp", "dp"), gain, gain, P(None, "dp"),
    )
    return jax.shard_map(body, mesh=mesh, in_specs=in_specs, out_specs=out_specs, check_vma=False)
```

```python
import functools

import jax
import jax.numpy as jnp
from jax import lax
from jax.experimental import pallas as pl
from jax.experimental.pallas import tpu as pltpu
from jax.experimental.layout import Layout, with_layout_constraint
from jax.sharding import PartitionSpec as P

HEADS = 32
KV = 4
HD = 64
HALF = HD // 2
EPS = 1e-05
F32 = jnp.float32
BF16 = jnp.bfloat16
SCALE = HD ** (-0.5)
NEG = -1e30


def dot(left, right, left_dim, right_dim):
    return lax.dot_general(
        left, right, (((left_dim,), (right_dim,)), ((), ())), preferred_element_type=F32
    )


def swap(values, bit, count, axis="sp"):
    return lax.ppermute(values, axis, [(i, i ^ bit) for i in range(count)])


def order_of(count):
    order = [0]
    bit = count // 2
    while bit:
        order += [member ^ bit for member in order]
        bit //= 2
    return order


def spread(block, count, axis="sp", stop=1):
    parts = list(block) if isinstance(block, (list, tuple)) else [block]
    bit = count // (2 * len(parts))
    while bit >= stop:
        parts += [swap(part, bit, count, axis) for part in parts]
        bit //= 2
    return parts


def after(values, *others):
    return lax.optimization_barrier((values,) + others)[0]


def gather_rows(block, count):
    return jnp.concatenate(spread(block, count), axis=0)


def halve(left, bit, count, axis="dp"):
    side = (lax.axis_index(axis) & bit) // bit
    pairs = left.reshape((left.shape[0] // 2, 2) + left.shape[1:])
    leaving = lax.dynamic_index_in_dim(pairs, 1 - side, 1, False)
    staying = lax.dynamic_index_in_dim(pairs, side, 1, False)
    return staying, swap(leaving, bit, count, axis)


def join(staying, got):
    return staying.astype(F32) + got.astype(F32)


def finish(left, bit, count, axis="dp"):
    kind = left.dtype
    while bit < count:
        left = join(*halve(left.astype(kind), bit, count, axis))
        bit *= 2
    return left[0].astype(F32)


def blocks_of(values, count):
    return values.reshape((count, values.shape[0] // count) + values.shape[1:])


def reduce_near(product, rows, count):
    half = rows // 2
    got = swap(product(half, rows).astype(BF16), 1, count)
    return product(0, half) + got.astype(F32)


def reduce_pair(keep, send, count):
    return keep.astype(F32) + swap(send, 1, count).astype(F32)


def reduce_far(left, count):
    bit = 2
    while bit < count:
        half = left.shape[0] // 2
        got = swap(left[half:].astype(BF16), bit, count)
        left = left[:half] + got.astype(F32)
        bit *= 2
    return left


def flip_blocks(values, count, to_absolute):
    me = lax.axis_index("sp")
    order = order_of(count)
    size = values.shape[-1] // count
    blocks = [values[..., j * size : (j + 1) * size] for j in range(count)]
    if to_absolute:
        blocks = [blocks[order.index(offset)] for offset in range(count)]
    bit = 1
    while bit < count:
        odd = (me & bit) != 0
        blocks = [jnp.where(odd, blocks[j ^ bit], blocks[j]) for j in range(count)]
        bit *= 2
    if not to_absolute:
        blocks = [blocks[offset] for offset in order]
    return jnp.concatenate(blocks, axis=-1)


def row_major(values):
    return with_layout_constraint(values, Layout(major_to_minor=tuple(range(values.ndim))))


def block_of(length):
    for size in (256, 128):
        if length % size == 0:
            return size
    return length


def forward_kernel(block, len_ref, q_ref, k_ref, v_ref, out_ref, lse_ref):
    full = q_ref.shape[-1]
    length = len_ref[0]
    key_at = lax.broadcasted_iota(jnp.int32, (block, block), 0)
    row_at = lax.broadcasted_iota(jnp.int32, (block, block), 1)
    for step in range(full // block):
        start = step * block
        here = slice(start, start + block)
        queries = q_ref[0, :, here]
        near = jnp.dot(k_ref[here, :], queries, preferred_element_type=F32)
        near = jnp.where((key_at <= row_at) & (key_at + start < length), near, NEG)
        top = jnp.max(near, axis=0, keepdims=True)
        if start:
            far = jnp.dot(k_ref[0:start, :], queries, preferred_element_type=F32)
            top = jnp.maximum(top, jnp.max(far, axis=0, keepdims=True))
        near = jnp.exp(near - top)
        total = jnp.sum(near, axis=0, keepdims=True)
        result = jnp.dot(v_ref[:, here], near.astype(BF16), preferred_element_type=F32)
        if start:
            far = jnp.exp(far - top)
            total = total + jnp.sum(far, axis=0, keepdims=True)
            result = result + jnp.dot(
                v_ref[:, 0:start], far.astype(BF16), preferred_element_type=F32
            )
        out_ref[0, :, here] = (result / total).astype(BF16)
        lse_ref[0, :, here] = top + jnp.log(total)


def attend_forward(queries, keys, values_t, length):
    heads, _, full = queries.shape
    block = block_of(full)
    return pl.pallas_call(
        functools.partial(forward_kernel, block),
        grid=(heads,),
        in_specs=[
            pl.BlockSpec(memory_space=pltpu.SMEM),
            pl.BlockSpec((1, HD, full), lambda h: (h, 0, 0)),
            pl.BlockSpec((full, HD), lambda h: (0, 0)),
            pl.BlockSpec((HD, full), lambda h: (0, 0)),
        ],
        out_specs=[
            pl.BlockSpec((1, HD, full), lambda h: (h, 0, 0)),
            pl.BlockSpec((1, 1, full), lambda h: (h, 0, 0)),
        ],
        out_shape=[
            jax.ShapeDtypeStruct((heads, HD, full), BF16),
            jax.ShapeDtypeStruct((heads, 1, full), F32),
        ],
        compiler_params=pltpu.CompilerParams(vmem_limit_bytes=48 * 2**20),
        cost_estimate=pl.CostEstimate(
            flops=heads * full * HD,
            bytes_accessed=heads * full * HD * 4,
            transcendentals=heads * full,
        ),
    )(length, queries, keys, values_t)


def backward_kernel(
    block, len_ref, q_ref, grad_ref, k_ref, kt_ref, v_ref, lse_ref, delta_ref, gq_ref, gk_ref, gv_ref, acc_ref
):
    full = q_ref.shape[-1]
    length = len_ref[0]

    @pl.when(pl.program_id(0) == 0)
    def _():
        gk_ref[...] = jnp.zeros_like(gk_ref)
        gv_ref[...] = jnp.zeros_like(gv_ref)

    key_at = lax.broadcasted_iota(jnp.int32, (block, block), 0)
    row_at = lax.broadcasted_iota(jnp.int32, (block, block), 1)
    for step in range(full // block):
        start = step * block
        here = slice(start, start + block)
        pieces = [(start, start + block, True)]
        if start + block < full:
            pieces.append((start + block, full, False))
        for low, high, edge in pieces:
            rows = slice(low, high)
            queries = q_ref[0, :, rows]
            grads = grad_ref[0, :, rows]
            scores = jnp.dot(k_ref[here, :], queries, preferred_element_type=F32)
            probs = jnp.exp(scores - lse_ref[0, :, rows])
            if edge:
                probs = jnp.where((key_at <= row_at) & (key_at + start < length), probs, 0.0)
            prob_grad = jnp.dot(v_ref[here, :], grads, preferred_element_type=F32)
            score_grad = (probs * (prob_grad - delta_ref[0, :, rows])).astype(BF16)
            gk_ref[here, :] += dot(score_grad, queries, 1, 1)
            gv_ref[here, :] += dot(probs.astype(BF16), grads, 1, 1)
            part = jnp.dot(kt_ref[:, here], score_grad, preferred_element_type=F32)
            if step == 0:
                acc_ref[:, rows] = part
            else:
                acc_ref[:, rows] += part
    gq_ref[0] = (acc_ref[...] * SCALE).astype(BF16)


def attend_backward(queries, grads, keys, keys_t, values, lse, delta, length):
    heads, _, full = queries.shape
    block = block_of(full)
    per_head = pl.BlockSpec((1, HD, full), lambda h: (h, 0, 0))
    per_row = pl.BlockSpec((1, 1, full), lambda h: (h, 0, 0))
    whole = pl.BlockSpec((full, HD), lambda h: (0, 0))
    return pl.pallas_call(
        functools.partial(backward_kernel, block),
        grid=(heads,),
        in_specs=[
            pl.BlockSpec(memory_space=pltpu.SMEM),
            per_head,
            per_head,
            whole,
            pl.BlockSpec((HD, full), lambda h: (0, 0)),
            whole,
            per_row,
            per_row,
        ],
        out_specs=[per_head, whole, whole],
        out_shape=[
            jax.ShapeDtypeStruct((heads, HD, full), BF16),
            jax.ShapeDtypeStruct((full, HD), F32),
            jax.ShapeDtypeStruct((full, HD), F32),
        ],
        scratch_shapes=[pltpu.VMEM((HD, full), F32)],
        compiler_params=pltpu.CompilerParams(vmem_limit_bytes=48 * 2**20),
        cost_estimate=pl.CostEstimate(
            flops=heads * full * HD,
            bytes_accessed=heads * full * HD * 6,
            transcendentals=heads * full,
        ),
    )(length, queries, grads, keys, keys_t, values, lse, delta)


TILE = 256


def tiles_of(hidden):
    if hidden % 128:
        return [(0, hidden)]
    return [(low, min(low + TILE, hidden)) for low in range(0, hidden, TILE)]


def interleave(gate, up):
    return jnp.concatenate(
        [array[:, low:high] for low, high in tiles_of(gate.shape[1]) for array in (gate, up)], axis=1
    )


def separate(both):
    pieces = tiles_of(both.shape[1] // 2)
    gate = [both[:, 2 * low : low + high] for low, high in pieces]
    up = [both[:, low + high : 2 * high] for low, high in pieces]
    return jnp.concatenate(gate, axis=1), jnp.concatenate(up, axis=1)


def activate(gate, up, grad):
    sig = 1.0 / (1.0 + jnp.exp(-gate))
    act = gate * sig
    slope = sig * (1.0 + gate * (1.0 - sig))
    return (act * up).astype(BF16), (grad * up * slope).astype(BF16), (grad * act).astype(BF16)


def copies_in(parts, buf_ref, sems):
    part = parts[0].shape[0]
    return [
        pltpu.make_async_copy(source, buf_ref.at[pl.ds(j * part, part)], sems.at[j])
        for j, source in enumerate(parts)
    ]


def by_tiles(run, last):
    step = pl.program_id(0)
    count = pl.num_programs(0)

    @pl.when(step == 0)
    def _():
        run(TILE, True)

    @pl.when((step > 0) & (step < count - 1))
    def _():
        run(TILE, False)

    @pl.when(step == count - 1)
    def _():
        run(last, False)


def hidden_grad_kernel(last, blocks, *refs):
    parts = refs[:blocks]
    down_ref, grad_ref, rows_out, rows_ref, in_sems, out_sem = refs[blocks:]
    part = parts[0].shape[0]
    coming = copies_in(parts, rows_ref, in_sems)
    leaving = pltpu.make_async_copy(rows_ref, rows_out, out_sem)

    def run(size, first):
        if first:
            for copy in coming:
                copy.start()
        for j in range(blocks):
            here = slice(j * part, (j + 1) * part)
            if first:
                coming[j].wait()
            grad_ref[here, :size] = jnp.dot(
                rows_ref[here, :], down_ref[:, :size], preferred_element_type=F32
            ).astype(BF16)
        if first:
            leaving.start()

    by_tiles(run, last)

    @pl.when(pl.program_id(0) == pl.num_programs(0) - 1)
    def _():
        leaving.wait()


def feed_kernel(last, blocks, *refs):
    parts = refs[:blocks]
    gu_ref, grad_ref, hid_ref, out_ref, rows_out, rows_ref, in_sems, out_sem = refs[blocks:]
    part = parts[0].shape[0]
    coming = copies_in(parts, rows_ref, in_sems)
    leaving = pltpu.make_async_copy(rows_ref, rows_out, out_sem)

    def run(size, first):
        if first:
            for copy in coming:
                copy.start()
        for j in range(blocks):
            here = slice(j * part, (j + 1) * part)
            if first:
                coming[j].wait()
            values = rows_ref[here, :]
            if size == TILE:
                gate = jnp.dot(values, gu_ref[:, :size], preferred_element_type=F32)
                up = jnp.dot(values, gu_ref[:, size : 2 * size], preferred_element_type=F32)
            else:
                both = jnp.dot(values, gu_ref[:, : 2 * size], preferred_element_type=F32)
                gate, up = both[:, :size], both[:, size:]
            grad = grad_ref[here, :size].astype(F32)
            hid, gate_grad, up_grad = activate(gate, up, grad)
            hid_ref[here, :size] = hid
            out_ref[here, :size] = gate_grad
            out_ref[here, size : 2 * size] = up_grad
        if first:
            leaving.start()

    by_tiles(run, last)

    @pl.when(pl.program_id(0) == pl.num_programs(0) - 1)
    def _():
        leaving.wait()


def tiled(hidden):
    return hidden % 128 == 0 and len(tiles_of(hidden)) >= 3


def row_scratch(rows, width, blocks):
    return [
        pltpu.VMEM((rows, width), BF16),
        pltpu.SemaphoreType.DMA((blocks,)),
        pltpu.SemaphoreType.DMA,
    ]


def hidden_grad(parts, down_t):
    blocks = len(parts)
    part, width = parts[0].shape
    rows = blocks * part
    hidden = down_t.shape[1]
    if not tiled(hidden):
        joined = jnp.concatenate(parts, axis=0)
        return dot(joined, down_t, 1, 0).astype(BF16), joined
    pieces = tiles_of(hidden)
    hbm = pl.BlockSpec(memory_space=pl.ANY)
    return pl.pallas_call(
        functools.partial(hidden_grad_kernel, pieces[-1][1] - pieces[-1][0], blocks),
        grid=(len(pieces),),
        in_specs=[hbm] * blocks + [pl.BlockSpec((width, TILE), lambda j: (0, j))],
        out_specs=[pl.BlockSpec((rows, TILE), lambda j: (0, j)), hbm],
        out_shape=[
            jax.ShapeDtypeStruct((rows, hidden), BF16),
            jax.ShapeDtypeStruct((rows, width), BF16),
        ],
        scratch_shapes=row_scratch(rows, width, blocks),
        compiler_params=pltpu.CompilerParams(vmem_limit_bytes=56 * 2**20),
        cost_estimate=pl.CostEstimate(
            flops=1000000, bytes_accessed=1000000, transcendentals=1000
        ),
    )(*parts, down_t)


def feed(parts, gu_w, grad):
    blocks = len(parts)
    part, width = parts[0].shape
    rows = blocks * part
    hidden = grad.shape[1]
    if not tiled(hidden):
        joined = jnp.concatenate(parts, axis=0)
        gate_w, up_w = separate(gu_w)
        hid, gate_grad, up_grad = activate(
            dot(joined, gate_w, 1, 0), dot(joined, up_w, 1, 0), grad.astype(F32)
        )
        return hid, interleave(gate_grad, up_grad), joined
    pieces = tiles_of(hidden)
    hbm = pl.BlockSpec(memory_space=pl.ANY)
    return pl.pallas_call(
        functools.partial(feed_kernel, pieces[-1][1] - pieces[-1][0], blocks),
        grid=(len(pieces),),
        in_specs=[hbm] * blocks
        + [
            pl.BlockSpec((width, 2 * TILE), lambda j: (0, j)),
            pl.BlockSpec((rows, TILE), lambda j: (0, j)),
        ],
        out_specs=[
            pl.BlockSpec((rows, TILE), lambda j: (0, j)),
            pl.BlockSpec((rows, 2 * TILE), lambda j: (0, j)),
            hbm,
        ],
        out_shape=[
            jax.ShapeDtypeStruct((rows, hidden), BF16),
            jax.ShapeDtypeStruct((rows, 2 * hidden), BF16),
            jax.ShapeDtypeStruct((rows, width), BF16),
        ],
        scratch_shapes=row_scratch(rows, width, blocks),
        compiler_params=pltpu.CompilerParams(vmem_limit_bytes=56 * 2**20),
        cost_estimate=pl.CostEstimate(
            flops=rows * width * hidden,
            bytes_accessed=4 * rows * width,
            transcendentals=rows,
        ),
    )(*parts, gu_w, grad)


def rotate(values, cos, sin):
    one, two = values[:, :HALF], values[:, HALF:]
    return jnp.concatenate([one * cos - two * sin, two * cos + one * sin], axis=1)


def rotate_back(grad, cos, sin):
    one, two = grad[:, :HALF], grad[:, HALF:]
    return jnp.concatenate([one * cos + two * sin, two * cos - one * sin], axis=1)


def fits(part):
    return part % 128 == 0


def place(at_ref, j, part):
    return pl.ds(pl.multiple_of(at_ref[j] * part, 128), part)


SMALL = pl.CostEstimate(flops=1000000, bytes_accessed=1000000, transcendentals=1000)
PARAMS = pltpu.CompilerParams(vmem_limit_bytes=56 * 2**20)
IN_HBM = pl.BlockSpec(memory_space=pl.ANY)
IN_VMEM = pl.BlockSpec(memory_space=pltpu.VMEM)
IN_SMEM = pl.BlockSpec(memory_space=pltpu.SMEM)


def fetch(parts, buf_ref, sems):
    part = parts[0].shape[0]
    return [
        pltpu.make_async_copy(source, buf_ref.at[pl.ds(j * part, part)], sems.at[j])
        for j, source in enumerate(parts)
    ]


def project_kernel(blocks, at_ref, *refs):
    parts = refs[:blocks]
    gain_ref, w_ref, cos_ref, sin_ref = refs[blocks : blocks + 4]
    n1_out, q_ref, kt_ref, vt_ref, k_ref, v_ref, buf_ref, in_sems, out_sems = refs[blocks + 4 :]
    part = parts[0].shape[0]
    heads = q_ref.shape[0]
    coming = fetch(parts, buf_ref, in_sems)
    for copy in coming:
        copy.start()
    leaving = []
    for j in range(blocks):
        coming[j].wait()
        for low in range(j * part, (j + 1) * part, 128):
            here = slice(low, low + 128)
            values = buf_ref[here, :].astype(F32)
            scale = lax.rsqrt(jnp.mean(values * values, axis=-1, keepdims=True) + EPS)
            buf_ref[here, :] = (values * scale * gain_ref[...]).astype(BF16)
        rows = pl.ds(j * part, part)
        leaving.append(pltpu.make_async_copy(buf_ref.at[rows], n1_out.at[rows], out_sems.at[j]))
        leaving[-1].start()
        proj = dot(w_ref[...], buf_ref[j * part : (j + 1) * part, :], 1, 1)
        cos = cos_ref[:, j * part : (j + 1) * part][None]
        sin = sin_ref[:, j * part : (j + 1) * part][None]
        there = place(at_ref, j, part)
        cut = heads * HD
        q = rotate(proj[:cut].reshape(heads, HD, part), cos, sin) * SCALE
        q_ref[:, :, there] = q.astype(BF16)
        k = rotate(proj[cut : cut + HD].reshape(1, HD, part), cos, sin)[0]
        v = proj[cut + HD :]
        kt_ref[:, there] = k.astype(BF16)
        vt_ref[:, there] = v.astype(BF16)
        k_ref[there, :] = k.T.astype(BF16)
        v_ref[there, :] = v.T.astype(BF16)
    for copy in leaving:
        copy.wait()


def project(parts, at, gain, w_t, cos, sin, heads):
    blocks = len(parts)
    part, width = parts[0].shape
    full = blocks * part
    if not fits(part):
        cut = heads * HD
        values = jnp.concatenate(parts, axis=0).astype(F32)
        scale = lax.rsqrt(jnp.mean(values * values, axis=-1, keepdims=True) + EPS)
        n1 = (values * scale * gain).astype(BF16)
        proj = dot(w_t, n1, 1, 1)
        q = rotate(proj[:cut].reshape(heads, HD, full), cos[None], sin[None]) * SCALE
        k = rotate(proj[cut : cut + HD].reshape(1, HD, full), cos[None], sin[None])
        both = jnp.concatenate([q.reshape(cut, full), k[0], proj[cut + HD :]], axis=0).astype(BF16)
        both = flip_blocks(both, blocks, True)
        k_t, v_t = both[cut : cut + HD], both[cut + HD :]
        return n1, both[:cut].reshape(heads, HD, full), k_t, v_t, k_t.T, v_t.T
    flat = jax.ShapeDtypeStruct((HD, full), BF16)
    tall = jax.ShapeDtypeStruct((full, HD), BF16)
    return pl.pallas_call(
        functools.partial(project_kernel, blocks),
        in_specs=[IN_SMEM] + [IN_HBM] * blocks + [IN_VMEM] * 4,
        out_specs=[IN_HBM] + [IN_VMEM] * 5,
        out_shape=[
            jax.ShapeDtypeStruct((full, width), BF16),
            jax.ShapeDtypeStruct((heads, HD, full), BF16),
            flat,
            flat,
            tall,
            tall,
        ],
        scratch_shapes=[
            pltpu.VMEM((full, width), BF16),
            pltpu.SemaphoreType.DMA((blocks,)),
            pltpu.SemaphoreType.DMA((blocks,)),
        ],
        compiler_params=PARAMS,
        cost_estimate=SMALL,
    )(at, *parts, gain, w_t, cos, sin)


def merge_kernel(blocks, at_ref, att_ref, w_ref, keep_ref, send_ref):
    part = att_ref.shape[1] // blocks
    for j in range(blocks):
        mine = att_ref[:, place(at_ref, j, part)]
        product = dot(mine, w_ref[...], 0, 0).astype(BF16)
        target, slot = (keep_ref, j) if j < blocks // 2 else (send_ref, j - blocks // 2)
        target[slot * part : (slot + 1) * part, :] = product


def merge_heads(att, at, out_w, blocks):
    cut, full = att.shape
    half = full // 2
    width = out_w.shape[1]
    if not fits(full // blocks):
        product = dot(flip_blocks(att, blocks, False), out_w, 0, 0).astype(BF16)
        return product[:half], product[half:]
    return pl.pallas_call(
        functools.partial(merge_kernel, blocks),
        in_specs=[IN_SMEM, IN_VMEM, IN_VMEM],
        out_specs=[IN_VMEM, IN_VMEM],
        out_shape=[jax.ShapeDtypeStruct((half, width), BF16)] * 2,
        compiler_params=PARAMS,
        cost_estimate=SMALL,
    )(at, att, out_w)


def split_kernel(blocks, has_sum, at_ref, *refs):
    parts = refs[:blocks]
    w_ref, att_ref = refs[blocks : blocks + 2]
    refs = refs[blocks + 2 :]
    if has_sum:
        sum_ref, refs = refs[0], refs[1:]
    grad_ref, delta_ref, wgrad_ref, buf_ref, acc_ref, sems = refs
    part = parts[0].shape[0]
    heads = att_ref.shape[0]
    coming = fetch(parts, buf_ref, sems)
    for copy in coming:
        copy.start()
    for j in range(blocks):
        coming[j].wait()
        rows = buf_ref[j * part : (j + 1) * part, :]
        there = place(at_ref, j, part)
        att = att_ref[:, :, there]
        grad = dot(w_ref[...], rows, 1, 1).astype(BF16).reshape(heads, HD, part)
        grad_ref[:, :, there] = grad
        delta_ref[:, :, there] = jnp.sum(
            grad.astype(F32) * att.astype(F32), axis=1, keepdims=True
        )
        share = jnp.dot(att.reshape(heads * HD, part), rows, preferred_element_type=F32)
        if j:
            acc_ref[...] += share
        elif has_sum:
            acc_ref[...] = sum_ref[...] + share
        else:
            acc_ref[...] = share
    wgrad_ref[...] = acc_ref[...].astype(wgrad_ref.dtype)


def split_heads(parts, at, out_w, att, so_far):
    blocks = len(parts)
    part, width = parts[0].shape
    heads, _, full = att.shape
    kind = F32 if so_far is None else BF16
    if not fits(part):
        rows = jnp.concatenate(parts, axis=0)
        grad = flip_blocks(dot(out_w, rows, 1, 1).astype(BF16), blocks, True)
        grad = grad.reshape(heads, HD, full)
        delta = jnp.sum(grad.astype(F32) * att.astype(F32), axis=1, keepdims=True)
        wgrad = dot(flip_blocks(att.reshape(heads * HD, full), blocks, False), rows, 1, 0)
        return grad, delta, (wgrad if so_far is None else so_far + wgrad).astype(kind)
    more = [] if so_far is None else [so_far]
    return pl.pallas_call(
        functools.partial(split_kernel, blocks, bool(more)),
        in_specs=[IN_SMEM] + [IN_HBM] * blocks + [IN_VMEM] * (2 + len(more)),
        out_specs=[IN_VMEM] * 3,
        out_shape=[
            jax.ShapeDtypeStruct((heads, HD, full), BF16),
            jax.ShapeDtypeStruct((heads, 1, full), F32),
            jax.ShapeDtypeStruct((heads * HD, width), kind),
        ],
        scratch_shapes=[
            pltpu.VMEM((full, width), BF16),
            pltpu.VMEM((heads * HD, width), F32),
            pltpu.SemaphoreType.DMA((blocks,)),
        ],
        compiler_params=PARAMS,
        cost_estimate=SMALL,
    )(at, *parts, out_w, att, *more)


def return_kernel(blocks, has_sum, at_ref, *refs):
    gq_ref, gk_ref, gv_ref, cos_ref, sin_ref, w_ref, n1_in = refs[:7]
    refs = refs[7:]
    if has_sum:
        sum_ref, refs = refs[0], refs[1:]
    keep_ref, send_ref, wgrad_ref, buf_ref, acc_ref, sems = refs
    heads, _, full = gq_ref.shape
    part = full // blocks
    coming = fetch([n1_in.at[pl.ds(j * part, part)] for j in range(blocks)], buf_ref, sems)
    for copy in coming:
        copy.start()
    for j in range(blocks):
        there = place(at_ref, j, part)
        cos = cos_ref[:, j * part : (j + 1) * part][None]
        sin = sin_ref[:, j * part : (j + 1) * part][None]
        gq = rotate_back(gq_ref[:, :, there].astype(F32), cos, sin)
        gk = rotate_back(gk_ref[there, :].T[None], cos, sin)[0]
        grad = jnp.concatenate(
            [
                gq.reshape(heads * HD, part).astype(BF16),
                gk.astype(BF16),
                gv_ref[there, :].T.astype(BF16),
            ],
            axis=0,
        )
        product = dot(grad, w_ref[...], 0, 0).astype(BF16)
        target, slot = (keep_ref, j) if j < blocks // 2 else (send_ref, j - blocks // 2)
        target[slot * part : (slot + 1) * part, :] = product
        coming[j].wait()
        share = jnp.dot(grad, buf_ref[j * part : (j + 1) * part, :], preferred_element_type=F32)
        if j:
            acc_ref[...] += share
        elif has_sum:
            acc_ref[...] = sum_ref[...] + share
        else:
            acc_ref[...] = share
    if has_sum:
        groups, _, columns = wgrad_ref.shape
        for d in range(groups):
            wgrad_ref[d] = acc_ref[:, d * columns : (d + 1) * columns].astype(BF16)
    else:
        wgrad_ref[...] = acc_ref[...]


def return_rows(gq, gk, gv, at, cos, sin, w_t, n1, so_far, groups):
    heads, _, full = gq.shape
    blocks = at.shape[0]
    columns, width = w_t.shape
    half = full // 2
    last = so_far is not None
    if not fits(full // blocks):
        back = jnp.concatenate([gq.reshape(heads * HD, full).astype(F32), gk.T, gv.T], axis=0)
        back = flip_blocks(back, blocks, False)
        turned = rotate_back(
            back[: heads * HD + HD].reshape(heads + 1, HD, full), cos[None], sin[None]
        )
        grad = jnp.concatenate(
            [turned.reshape(heads * HD + HD, full), back[heads * HD + HD :]], axis=0
        ).astype(BF16)
        product = dot(grad, w_t, 0, 0).astype(BF16)
        wgrad = dot(grad, n1, 1, 0)
        if last:
            wgrad = (so_far + wgrad).astype(BF16)
            wgrad = wgrad.reshape(columns, groups, width // groups).transpose(1, 0, 2)
        return product[:half], product[half:], wgrad
    more = [so_far] if last else []
    shape = (groups, columns, width // groups) if last else (columns, width)
    return pl.pallas_call(
        functools.partial(return_kernel, blocks, last),
        in_specs=[IN_SMEM] + [IN_VMEM] * 6 + [IN_HBM] + [IN_VMEM] * len(more),
        out_specs=[IN_VMEM] * 3,
        out_shape=[
            jax.ShapeDtypeStruct((half, width), BF16),
            jax.ShapeDtypeStruct((half, width), BF16),
            jax.ShapeDtypeStruct(shape, BF16 if last else F32),
        ],
        scratch_shapes=[
            pltpu.VMEM((full, width), BF16),
            pltpu.VMEM((columns, width), F32),
            pltpu.SemaphoreType.DMA((blocks,)),
        ],
        compiler_params=PARAMS,
        cost_estimate=SMALL,
    )(at, gq, gk, gv, cos, sin, w_t, n1, *more)


def body(
    tokens,
    cotangent,
    lengths,
    query_weight,
    key_weight,
    value_weight,
    output_weight,
    gate_weight,
    up_weight,
    down_weight,
    attention_gain,
    feed_gain,
):
    seqs, local, width = tokens.shape
    sp = lax.axis_size("sp")
    dp = lax.axis_size("dp")
    me = lax.axis_index("sp")
    full = local * sp
    heads = HEADS // sp
    own_rows = query_weight.shape[0]
    dp_rows = own_rows * sp
    q_cols = heads * HD
    order = order_of(sp)
    hidden = gate_weight.shape[1]

    positions = me * local + jnp.arange(local)
    valid = positions[None, :] < lengths[:, None]

    def pick(array, target):
        head = target * KV // sp
        return array[:, head * HD : (head + 1) * HD]

    extra = jnp.concatenate(
        [attention_gain[:, None], feed_gain[:, None], jnp.zeros((own_rows, 126), BF16)], axis=1
    )
    to_send = jnp.stack(
        [
            jnp.concatenate(
                [
                    query_weight[:, t * q_cols : (t + 1) * q_cols],
                    pick(key_weight, t),
                    pick(value_weight, t),
                    extra,
                ],
                axis=1,
            )
            for t in range(sp)
        ]
    )
    proj_cols = q_cols + 2 * HD
    in_block = lax.all_to_all(to_send, "sp", 0, 0, tiled=True).reshape(dp_rows, proj_cols + 128)
    total = dp * sp
    there = [(n, (n % dp) * sp + n // dp) for n in range(total)]
    back = [(b, a) for a, b in there]
    out_block = lax.ppermute(output_weight, ("dp", "sp"), there)
    out_cols = own_rows * width // dp_rows
    attn_mine = jnp.concatenate([in_block, out_block.reshape(dp_rows, out_cols)], axis=1)
    attn_all = row_major(lax.all_gather(row_major(attn_mine), "dp", axis=0, tiled=True))
    there_is = jnp.isfinite(in_block[0, 0].astype(F32))

    def later(array):
        return jnp.where(there_is, array, jnp.zeros_like(array))

    half = dp // 2
    gu_mine = interleave(gate_weight, up_weight)
    down_t = row_major(lax.all_gather(row_major(down_weight.T), "dp", axis=0, tiled=True))
    gu_w = row_major(
        lax.all_gather(row_major(after(gu_mine, attn_all)), "dp", axis=0, tiled=True)
    )
    held = later(tokens)
    cot_local = jnp.where(valid[..., None], cotangent, jnp.zeros_like(cotangent))
    rows_far = []
    chain = []
    for s in range(seqs):
        rows_far.append(spread(after(held[s], *chain), sp, "sp", 2))
        chain = rows_far[-1][1:]
    rows_all = [spread(far, sp) for far in rows_far]
    cot_far = [spread(after(cot_local[0], *chain), sp, "sp", 2)]
    proj_t = attn_all[:, :proj_cols].T
    gains = attn_all[:, proj_cols : proj_cols + 2].astype(F32)
    gain_one, gain_two = gains[:, 0], gains[:, 1]
    out_w = attn_all[:, proj_cols + 128 :].reshape(q_cols, width)
    rows_all[0][0] = after(rows_all[0][0], *rows_far[-1])

    row_pos = jnp.concatenate([(me ^ member) * local + jnp.arange(local) for member in order])
    frequency = jnp.power(10000.0, -2.0 * jnp.arange(HALF).astype(F32) / HD)
    angles = frequency[:, None] * row_pos.astype(F32)[None, :]
    cos, sin = jnp.cos(angles), jnp.sin(angles)
    at = jnp.stack([me ^ member for member in order]).astype(jnp.int32)

    def norm(values, gain):
        scale = lax.rsqrt(jnp.mean(values * values, axis=-1, keepdims=True) + EPS)
        return values * scale * gain

    def norm_back(grad, values, gain):
        scale = lax.rsqrt(jnp.mean(values * values, axis=-1, keepdims=True) + EPS)
        scaled = grad * gain
        return scale * scaled - values * scale**3 * jnp.mean(scaled * values, axis=-1, keepdims=True)

    normed_one, saved, branches, middles, n2_far, begins = [], [], [], [], [], []

    def take_branch(s, mark):
        branch = after(reduce_far(begins[s], sp), mark)
        middle = tokens[s].astype(F32) + branch
        n2_far.append(spread(norm(middle, gain_two).astype(BF16), sp, "sp", 2))
        branches.append(branch)
        middles.append(middle)

    for s in range(seqs):
        parts = list(rows_all[s])
        if s:
            parts[0] = after(parts[0], begins[-1])
        n1, q, k_t, v_t, k, v = project(parts, at, gain_one[None], proj_t, cos, sin, heads)
        normed_one.append(n1)
        att, lse = attend_forward(q, k, v_t, lengths[s : s + 1])
        flat = att.reshape(q_cols, full)
        if s == 0:
            flat = after(flat, *cot_far[0], down_t)
        else:
            take_branch(s - 1, att)
            flat = after(flat, *n2_far[-1])
        begins.append(reduce_pair(*merge_heads(flat, at, out_w, sp), sp))
        saved.append((q, k, k_t, v, att, lse))
    for s in range(1, seqs):
        cot_far.append(spread(after(cot_local[s], begins[-1]), sp, "sp", 2))
    hidden_grads, cot_all = zip(*[hidden_grad(spread(far, sp), down_t) for far in cot_far])
    gu_w = after(gu_w, *hidden_grads)
    take_branch(seqs - 1, gu_w)
    begun = begins[-1]
    normed_two = [spread(n2_far[0], sp)]

    def mlp_near(hid):
        return reduce_near(lambda lo, hi: dot(hid[lo:hi], down_t, 1, 1), full, sp)

    begun_mixed = []
    hiddens, gu_grads, n2_grads, middle_grads, grad_rows = [], [], [], [], []
    down_wgrad = 0.0
    for s in range(seqs):
        n2 = [after(part, begun, *hidden_grads) for part in normed_two[s]]
        hid, gu_grad, joined = feed(n2, gu_w, hidden_grads[s])
        normed_two[s] = joined
        hiddens.append(hid)
        gu_grads.append(gu_grad)
        if s < seqs - 1:
            low, high = [n2_far[s + 1][0]], n2_far[s + 1]
            hid = after(hid, *low)
            down_wgrad = row_major(dot(cot_all[s], hid, 0, 0))
            begun_mixed.append(mlp_near(hid))
            high = high + [down_wgrad, begun_mixed[0]]
        else:
            low, high = [n2_grads[0]], [n2_grads[0]]
        send, keep = after(gu_grad, *low), after(gu_grad, *high)
        begun = reduce_near(
            lambda lo, hi: dot((keep if lo == 0 else send)[lo:hi], gu_w, 1, 1), full, sp
        )
        n2_grads.append(reduce_far(begun, sp))
        if s < seqs - 1:
            normed_two.append(spread(n2_far[s + 1], sp))
    gu_wgrad = 0.0
    for s in range(seqs):
        held = after(n2_grads[s], gu_grads[-1]) if s == 0 else after(n2_grads[s], gu_wgrad)
        middle_grads.append(cot_local[s].astype(F32) + norm_back(held, middles[s], gain_two))
        parts = spread(middle_grads[s].astype(BF16), sp, "sp", 2)
        far_rows = parts[1:]
        if s == 0:
            gu_wgrad = dot(after(normed_two[0], begun, middle_grads[0]), gu_grads[0], 0, 0)
            parts = [after(part, gu_wgrad) for part in parts]
        grad_rows.append(spread(parts, sp))
        if s == 0:
            for t in range(1, seqs):
                gu_wgrad = gu_wgrad + dot(after(normed_two[t], *grad_rows[0]), gu_grads[t], 0, 0)
            gu_wgrad = gu_wgrad.astype(BF16)
    rows = after(cot_all[-1], middle_grads[-1])
    down_wgrad = down_wgrad + dot(rows, hiddens[-1], 0, 0)
    down_wgrad = down_wgrad.astype(BF16)
    hid = after(hiddens[-1], down_wgrad, *far_rows)
    begun_mixed.append(mlp_near(hid))

    feed_wgrad = jnp.concatenate([gu_wgrad, down_wgrad], axis=1)
    feed_grad = row_major(
        lax.psum_scatter(row_major(feed_wgrad), "dp", scatter_dimension=0, tiled=True)
    )

    def norm_sums(mixed):
        sums = jnp.stack(
            [
                jnp.stack(
                    [
                        jnp.sum(jnp.where(valid[s][:, None], member[s] * member[s], 0.0))
                        for s in range(seqs)
                    ]
                )
                for member in ([tokens[s].astype(F32) for s in range(seqs)], branches, mixed)
            ]
        )
        return sums

    proj_wgrad = None
    out_wgrad = None
    input_grads = []
    for s in range(seqs):
        q, k, k_t, v, att, lse = saved[s]
        rows = list(grad_rows[s])
        rows[0] = after(rows[0], mark) if s else after(rows[0], *begun_mixed)
        att_grad, delta, out_wgrad = split_heads(rows, at, out_w, att, out_wgrad)
        if s:
            q = after(q, begun)
            staying, got = halve(blocks_of(out_wgrad, dp), 1, dp)
        gq, gk, gv = attend_backward(q, att_grad, k, k_t, v, lse, delta, lengths[s : s + 1])
        mark = gq
        if s == 0:
            mixed = [reduce_far(after(begun_mixed[0], *far_rows), sp)]
            gq = after(gq, mixed[0])
            mixed += [reduce_far(after(begun_mixed[t], mark), sp) for t in range(1, seqs)]
        else:
            sums = norm_sums(mixed)
            gq = after(gq, got, *mixed, n1_grad)
        keep, send, proj_wgrad = return_rows(
            gq, gk, gv, at, cos, sin, proj_t, normed_one[s], proj_wgrad, dp
        )
        begun = reduce_pair(keep, send, sp)
        if s == 0:
            n1_grad = reduce_far(begun, sp)
        else:
            out_left = join(staying, after(got, mark)).astype(BF16)
            out_staying, out_got = halve(out_left, 2, dp)
            n1_grad = reduce_far(begun, sp)
        rest = norm_back(n1_grad, tokens[s].astype(F32), gain_one)
        input_grads.append((middle_grads[s] + rest).astype(BF16))
    input_grad = jnp.stack(input_grads)
    staying, got = halve(proj_wgrad, 1, dp)
    left = join(staying, after(got, begun)).astype(BF16)
    out_left = join(out_staying, after(out_got, left)).astype(BF16)
    staying, got = halve(left, 2, dp)
    left = join(staying, after(got, n1_grad, feed_grad)).astype(BF16)
    proj_grad = finish(left, 4, dp)
    out_grad = finish(after(out_left, left), 4, dp)
    out_grad = lax.ppermute(out_grad.astype(BF16), ("dp", "sp"), back).astype(F32)
    feed_grad = after(feed_grad, left).astype(F32)
    gate_out, up_out = separate(feed_grad[:, : 2 * hidden])
    down_out = feed_grad[:, 2 * hidden :].T

    block_out = jnp.stack(
        [((middles[s] + mixed[s]) * valid[s][:, None]).astype(BF16) for s in range(seqs)]
    )
    proj_grad = proj_grad.astype(BF16).reshape(proj_cols, sp, own_rows).transpose(1, 0, 2)
    proj_grad = lax.all_to_all(proj_grad, "sp", 0, 0, tiled=True).astype(F32)
    query_grad = proj_grad[:, :q_cols].transpose(2, 0, 1).reshape(own_rows, HEADS * HD)

    def kv_grad(array):
        copies = array.reshape(KV, sp // KV, HD, own_rows).sum(axis=1)
        return copies.transpose(2, 0, 1).reshape(own_rows, KV * HD)

    key_grad = kv_grad(proj_grad[:, q_cols : q_cols + HD])
    value_grad = kv_grad(proj_grad[:, q_cols + HD :])

    def rowwise(weight, grad):
        return jnp.sum(weight.astype(F32) * grad, axis=1)

    gain_one_grad = (
        rowwise(query_weight, query_grad)
        + rowwise(key_weight, key_grad)
        + rowwise(value_weight, value_grad)
    ) / attention_gain.astype(F32)
    shares = rowwise(gate_weight, gate_out) + rowwise(up_weight, up_out)
    gain_two_grad = finish(blocks_of(shares, sp), 1, sp, "sp") / feed_gain.astype(F32)

    sums = after(sums, n1_grad)
    bit = 1
    while bit < sp:
        sums = sums + swap(sums, bit, sp)
        bit *= 2
    branch_norms = jnp.sqrt(sums / (lengths.astype(F32) * width))
    return (
        block_out,
        input_grad,
        query_grad,
        key_grad,
        value_grad,
        out_grad,
        gate_out,
        up_out,
        down_out,
        gain_one_grad,
        gain_two_grad,
        branch_norms,
    )


def solution(mesh):
    rows = P(("dp", "sp"), None)
    gain = P(("dp", "sp"))
    seq = P("dp", "sp", None)
    in_specs = (
        seq, seq, P("dp"), rows, rows, rows, rows,
        P("dp", "sp"), P("dp", "sp"), P("sp", "dp"), gain, gain,
    )
    out_specs = (
        seq, seq, rows, rows, rows, rows,
        P("dp", "sp"), P("dp", "sp"), P("sp", "dp"), gain, gain, P(None, "dp"),
    )
    return jax.shard_map(body, mesh=mesh, in_specs=in_specs, out_specs=out_specs, check_vma=False)
```

```python
import functools

import jax
import jax.numpy as jnp
from jax import lax
from jax.experimental import pallas as pl
from jax.experimental.pallas import tpu as pltpu
from jax.experimental.layout import Layout, with_layout_constraint
from jax.sharding import PartitionSpec as P

HEADS = 32
KV = 4
HD = 64
HALF = HD // 2
EPS = 1e-05
F32 = jnp.float32
BF16 = jnp.bfloat16
SCALE = HD ** (-0.5)
NEG = -1e30


def dot(left, right, left_dim, right_dim):
    return lax.dot_general(
        left, right, (((left_dim,), (right_dim,)), ((), ())), preferred_element_type=F32
    )


def swap(values, bit, count, axis="sp"):
    return lax.ppermute(values, axis, [(i, i ^ bit) for i in range(count)])


def order_of(count):
    order = [0]
    bit = count // 2
    while bit:
        order += [member ^ bit for member in order]
        bit //= 2
    return order


def spread(block, count, axis="sp", stop=1):
    parts = list(block) if isinstance(block, (list, tuple)) else [block]
    bit = count // (2 * len(parts))
    while bit >= stop:
        parts += [swap(part, bit, count, axis) for part in parts]
        bit //= 2
    return parts


def after(values, *others):
    return lax.optimization_barrier((values,) + others)[0]


def gather_rows(block, count):
    return jnp.concatenate(spread(block, count), axis=0)


def halve(left, bit, count, axis="dp"):
    side = (lax.axis_index(axis) & bit) // bit
    pairs = left.reshape((left.shape[0] // 2, 2) + left.shape[1:])
    leaving = lax.dynamic_index_in_dim(pairs, 1 - side, 1, False)
    staying = lax.dynamic_index_in_dim(pairs, side, 1, False)
    return staying, swap(leaving, bit, count, axis)


def join(staying, got):
    return staying.astype(F32) + got.astype(F32)


def finish(left, bit, count, axis="dp"):
    kind = left.dtype
    while bit < count:
        left = join(*halve(left.astype(kind), bit, count, axis))
        bit *= 2
    return left[0].astype(F32)


def blocks_of(values, count):
    return values.reshape((count, values.shape[0] // count) + values.shape[1:])


def reduce_near(product, rows, count):
    half = rows // 2
    got = swap(product(half, rows).astype(BF16), 1, count)
    return product(0, half) + got.astype(F32)


def reduce_pair(keep, send, count):
    return keep.astype(F32) + swap(send, 1, count).astype(F32)


def reduce_far(left, count):
    bit = 2
    while bit < count:
        half = left.shape[0] // 2
        got = swap(left[half:].astype(BF16), bit, count)
        left = left[:half] + got.astype(F32)
        bit *= 2
    return left


def flip_blocks(values, count, to_absolute):
    me = lax.axis_index("sp")
    order = order_of(count)
    size = values.shape[-1] // count
    blocks = [values[..., j * size : (j + 1) * size] for j in range(count)]
    if to_absolute:
        blocks = [blocks[order.index(offset)] for offset in range(count)]
    bit = 1
    while bit < count:
        odd = (me & bit) != 0
        blocks = [jnp.where(odd, blocks[j ^ bit], blocks[j]) for j in range(count)]
        bit *= 2
    if not to_absolute:
        blocks = [blocks[offset] for offset in order]
    return jnp.concatenate(blocks, axis=-1)


def row_major(values):
    return with_layout_constraint(values, Layout(major_to_minor=tuple(range(values.ndim))))


def block_of(length):
    for size in (256, 128):
        if length % size == 0:
            return size
    return length


def forward_kernel(block, len_ref, q_ref, k_ref, v_ref, out_ref, lse_ref):
    full = q_ref.shape[-1]
    length = len_ref[0]
    key_at = lax.broadcasted_iota(jnp.int32, (block, block), 0)
    row_at = lax.broadcasted_iota(jnp.int32, (block, block), 1)
    for step in range(full // block):
        start = step * block
        here = slice(start, start + block)
        queries = q_ref[0, :, here]
        near = jnp.dot(k_ref[here, :], queries, preferred_element_type=F32)
        near = jnp.where((key_at <= row_at) & (key_at + start < length), near, NEG)
        top = jnp.max(near, axis=0, keepdims=True)
        if start:
            far = jnp.dot(k_ref[0:start, :], queries, preferred_element_type=F32)
            top = jnp.maximum(top, jnp.max(far, axis=0, keepdims=True))
        near = jnp.exp(near - top)
        total = jnp.sum(near, axis=0, keepdims=True)
        result = jnp.dot(v_ref[:, here], near.astype(BF16), preferred_element_type=F32)
        if start:
            far = jnp.exp(far - top)
            total = total + jnp.sum(far, axis=0, keepdims=True)
            result = result + jnp.dot(
                v_ref[:, 0:start], far.astype(BF16), preferred_element_type=F32
            )
        out_ref[0, :, here] = (result / total).astype(BF16)
        lse_ref[0, :, here] = top + jnp.log(total)


def attend_forward(queries, keys, values_t, length):
    heads, _, full = queries.shape
    block = block_of(full)
    return pl.pallas_call(
        functools.partial(forward_kernel, block),
        grid=(heads,),
        in_specs=[
            pl.BlockSpec(memory_space=pltpu.SMEM),
            pl.BlockSpec((1, HD, full), lambda h: (h, 0, 0)),
            pl.BlockSpec((full, HD), lambda h: (0, 0)),
            pl.BlockSpec((HD, full), lambda h: (0, 0)),
        ],
        out_specs=[
            pl.BlockSpec((1, HD, full), lambda h: (h, 0, 0)),
            pl.BlockSpec((1, 1, full), lambda h: (h, 0, 0)),
        ],
        out_shape=[
            jax.ShapeDtypeStruct((heads, HD, full), BF16),
            jax.ShapeDtypeStruct((heads, 1, full), F32),
        ],
        compiler_params=pltpu.CompilerParams(vmem_limit_bytes=48 * 2**20),
        cost_estimate=pl.CostEstimate(
            flops=heads * full * HD,
            bytes_accessed=heads * full * HD * 4,
            transcendentals=heads * full,
        ),
    )(length, queries, keys, values_t)


def backward_kernel(
    block, len_ref, q_ref, grad_ref, k_ref, kt_ref, v_ref, lse_ref, delta_ref, gq_ref, gk_ref, gv_ref, acc_ref
):
    full = q_ref.shape[-1]
    length = len_ref[0]

    @pl.when(pl.program_id(0) == 0)
    def _():
        gk_ref[...] = jnp.zeros_like(gk_ref)
        gv_ref[...] = jnp.zeros_like(gv_ref)

    key_at = lax.broadcasted_iota(jnp.int32, (block, block), 0)
    row_at = lax.broadcasted_iota(jnp.int32, (block, block), 1)
    for step in range(full // block):
        start = step * block
        here = slice(start, start + block)
        pieces = [(start, start + block, True)]
        if start + block < full:
            pieces.append((start + block, full, False))
        for low, high, edge in pieces:
            rows = slice(low, high)
            queries = q_ref[0, :, rows]
            grads = grad_ref[0, :, rows]
            scores = jnp.dot(k_ref[here, :], queries, preferred_element_type=F32)
            probs = jnp.exp(scores - lse_ref[0, :, rows])
            if edge:
                probs = jnp.where((key_at <= row_at) & (key_at + start < length), probs, 0.0)
            prob_grad = jnp.dot(v_ref[here, :], grads, preferred_element_type=F32)
            score_grad = (probs * (prob_grad - delta_ref[0, :, rows])).astype(BF16)
            gk_ref[here, :] += dot(score_grad, queries, 1, 1)
            gv_ref[here, :] += dot(probs.astype(BF16), grads, 1, 1)
            part = jnp.dot(kt_ref[:, here], score_grad, preferred_element_type=F32)
            if step == 0:
                acc_ref[:, rows] = part
            else:
                acc_ref[:, rows] += part
    gq_ref[0] = (acc_ref[...] * SCALE).astype(BF16)


def attend_backward(queries, grads, keys, keys_t, values, lse, delta, length):
    heads, _, full = queries.shape
    block = block_of(full)
    per_head = pl.BlockSpec((1, HD, full), lambda h: (h, 0, 0))
    per_row = pl.BlockSpec((1, 1, full), lambda h: (h, 0, 0))
    whole = pl.BlockSpec((full, HD), lambda h: (0, 0))
    return pl.pallas_call(
        functools.partial(backward_kernel, block),
        grid=(heads,),
        in_specs=[
            pl.BlockSpec(memory_space=pltpu.SMEM),
            per_head,
            per_head,
            whole,
            pl.BlockSpec((HD, full), lambda h: (0, 0)),
            whole,
            per_row,
            per_row,
        ],
        out_specs=[per_head, whole, whole],
        out_shape=[
            jax.ShapeDtypeStruct((heads, HD, full), BF16),
            jax.ShapeDtypeStruct((full, HD), F32),
            jax.ShapeDtypeStruct((full, HD), F32),
        ],
        scratch_shapes=[pltpu.VMEM((HD, full), F32)],
        compiler_params=pltpu.CompilerParams(vmem_limit_bytes=48 * 2**20),
        cost_estimate=pl.CostEstimate(
            flops=heads * full * HD,
            bytes_accessed=heads * full * HD * 6,
            transcendentals=heads * full,
        ),
    )(length, queries, grads, keys, keys_t, values, lse, delta)


TILE = 256


def tiles_of(hidden):
    if hidden % 128:
        return [(0, hidden)]
    return [(low, min(low + TILE, hidden)) for low in range(0, hidden, TILE)]


def interleave(gate, up):
    return jnp.concatenate(
        [array[:, low:high] for low, high in tiles_of(gate.shape[1]) for array in (gate, up)], axis=1
    )


def separate(both):
    pieces = tiles_of(both.shape[1] // 2)
    gate = [both[:, 2 * low : low + high] for low, high in pieces]
    up = [both[:, low + high : 2 * high] for low, high in pieces]
    return jnp.concatenate(gate, axis=1), jnp.concatenate(up, axis=1)


def activate(gate, up, grad):
    sig = 1.0 / (1.0 + jnp.exp(-gate))
    act = gate * sig
    slope = sig * (1.0 + gate * (1.0 - sig))
    return (act * up).astype(BF16), (grad * up * slope).astype(BF16), (grad * act).astype(BF16)


def copies_in(parts, buf_ref, sems):
    part = parts[0].shape[0]
    return [
        pltpu.make_async_copy(source, buf_ref.at[pl.ds(j * part, part)], sems.at[j])
        for j, source in enumerate(parts)
    ]


def by_tiles(run, last):
    step = pl.program_id(0)
    count = pl.num_programs(0)

    @pl.when(step == 0)
    def _():
        run(TILE, True)

    @pl.when((step > 0) & (step < count - 1))
    def _():
        run(TILE, False)

    @pl.when(step == count - 1)
    def _():
        run(last, False)


def hidden_grad_kernel(last, blocks, *refs):
    parts = refs[:blocks]
    down_ref, grad_ref, rows_out, rows_ref, in_sems, out_sem = refs[blocks:]
    part = parts[0].shape[0]
    coming = copies_in(parts, rows_ref, in_sems)
    leaving = pltpu.make_async_copy(rows_ref, rows_out, out_sem)

    def run(size, first):
        if first:
            for copy in coming:
                copy.start()
        for j in range(blocks):
            here = slice(j * part, (j + 1) * part)
            if first:
                coming[j].wait()
            grad_ref[here, :size] = jnp.dot(
                rows_ref[here, :], down_ref[:, :size], preferred_element_type=F32
            ).astype(BF16)
        if first:
            leaving.start()

    by_tiles(run, last)

    @pl.when(pl.program_id(0) == pl.num_programs(0) - 1)
    def _():
        leaving.wait()


def feed_kernel(last, blocks, *refs):
    parts = refs[:blocks]
    gu_ref, grad_ref, hid_ref, out_ref, rows_out, rows_ref, in_sems, out_sem = refs[blocks:]
    part = parts[0].shape[0]
    coming = copies_in(parts, rows_ref, in_sems)
    leaving = pltpu.make_async_copy(rows_ref, rows_out, out_sem)

    def run(size, first):
        if first:
            for copy in coming:
                copy.start()
        for j in range(blocks):
            here = slice(j * part, (j + 1) * part)
            if first:
                coming[j].wait()
            values = rows_ref[here, :]
            if size == TILE:
                gate = jnp.dot(values, gu_ref[:, :size], preferred_element_type=F32)
                up = jnp.dot(values, gu_ref[:, size : 2 * size], preferred_element_type=F32)
            else:
                both = jnp.dot(values, gu_ref[:, : 2 * size], preferred_element_type=F32)
                gate, up = both[:, :size], both[:, size:]
            grad = grad_ref[here, :size].astype(F32)
            hid, gate_grad, up_grad = activate(gate, up, grad)
            hid_ref[here, :size] = hid
            out_ref[here, :size] = gate_grad
            out_ref[here, size : 2 * size] = up_grad
        if first:
            leaving.start()

    by_tiles(run, last)

    @pl.when(pl.program_id(0) == pl.num_programs(0) - 1)
    def _():
        leaving.wait()


def tiled(hidden):
    return hidden % 128 == 0 and len(tiles_of(hidden)) >= 3


def row_scratch(rows, width, blocks):
    return [
        pltpu.VMEM((rows, width), BF16),
        pltpu.SemaphoreType.DMA((blocks,)),
        pltpu.SemaphoreType.DMA,
    ]


def hidden_grad(parts, down_t):
    blocks = len(parts)
    part, width = parts[0].shape
    rows = blocks * part
    hidden = down_t.shape[1]
    if not tiled(hidden):
        joined = jnp.concatenate(parts, axis=0)
        return dot(joined, down_t, 1, 0).astype(BF16), joined
    pieces = tiles_of(hidden)
    hbm = pl.BlockSpec(memory_space=pl.ANY)
    return pl.pallas_call(
        functools.partial(hidden_grad_kernel, pieces[-1][1] - pieces[-1][0], blocks),
        grid=(len(pieces),),
        in_specs=[hbm] * blocks + [pl.BlockSpec((width, TILE), lambda j: (0, j))],
        out_specs=[pl.BlockSpec((rows, TILE), lambda j: (0, j)), hbm],
        out_shape=[
            jax.ShapeDtypeStruct((rows, hidden), BF16),
            jax.ShapeDtypeStruct((rows, width), BF16),
        ],
        scratch_shapes=row_scratch(rows, width, blocks),
        compiler_params=pltpu.CompilerParams(vmem_limit_bytes=56 * 2**20),
        cost_estimate=pl.CostEstimate(
            flops=1000000, bytes_accessed=1000000, transcendentals=1000
        ),
    )(*parts, down_t)


def feed(parts, gu_w, grad):
    blocks = len(parts)
    part, width = parts[0].shape
    rows = blocks * part
    hidden = grad.shape[1]
    if not tiled(hidden):
        joined = jnp.concatenate(parts, axis=0)
        gate_w, up_w = separate(gu_w)
        hid, gate_grad, up_grad = activate(
            dot(joined, gate_w, 1, 0), dot(joined, up_w, 1, 0), grad.astype(F32)
        )
        return hid, interleave(gate_grad, up_grad), joined
    pieces = tiles_of(hidden)
    hbm = pl.BlockSpec(memory_space=pl.ANY)
    return pl.pallas_call(
        functools.partial(feed_kernel, pieces[-1][1] - pieces[-1][0], blocks),
        grid=(len(pieces),),
        in_specs=[hbm] * blocks
        + [
            pl.BlockSpec((width, 2 * TILE), lambda j: (0, j)),
            pl.BlockSpec((rows, TILE), lambda j: (0, j)),
        ],
        out_specs=[
            pl.BlockSpec((rows, TILE), lambda j: (0, j)),
            pl.BlockSpec((rows, 2 * TILE), lambda j: (0, j)),
            hbm,
        ],
        out_shape=[
            jax.ShapeDtypeStruct((rows, hidden), BF16),
            jax.ShapeDtypeStruct((rows, 2 * hidden), BF16),
            jax.ShapeDtypeStruct((rows, width), BF16),
        ],
        scratch_shapes=row_scratch(rows, width, blocks),
        compiler_params=pltpu.CompilerParams(vmem_limit_bytes=56 * 2**20),
        cost_estimate=pl.CostEstimate(
            flops=rows * width * hidden,
            bytes_accessed=4 * rows * width,
            transcendentals=rows,
        ),
    )(*parts, gu_w, grad)


def rotate(values, cos, sin):
    one, two = values[:, :HALF], values[:, HALF:]
    return jnp.concatenate([one * cos - two * sin, two * cos + one * sin], axis=1)


def rotate_back(grad, cos, sin):
    one, two = grad[:, :HALF], grad[:, HALF:]
    return jnp.concatenate([one * cos + two * sin, two * cos - one * sin], axis=1)


def fits(part):
    return part % 128 == 0


def place(at_ref, j, part):
    return pl.ds(pl.multiple_of(at_ref[j] * part, 128), part)


SMALL = pl.CostEstimate(flops=1000000, bytes_accessed=1000000, transcendentals=1000)
PARAMS = pltpu.CompilerParams(vmem_limit_bytes=56 * 2**20)
IN_HBM = pl.BlockSpec(memory_space=pl.ANY)
IN_VMEM = pl.BlockSpec(memory_space=pltpu.VMEM)
IN_SMEM = pl.BlockSpec(memory_space=pltpu.SMEM)


def fetch(parts, buf_ref, sems):
    part = parts[0].shape[0]
    return [
        pltpu.make_async_copy(source, buf_ref.at[pl.ds(j * part, part)], sems.at[j])
        for j, source in enumerate(parts)
    ]


def project_kernel(blocks, at_ref, *refs):
    parts = refs[:blocks]
    gain_ref, w_ref, cos_ref, sin_ref = refs[blocks : blocks + 4]
    n1_out, q_ref, kt_ref, vt_ref, k_ref, v_ref, buf_ref, in_sems, out_sems = refs[blocks + 4 :]
    part = parts[0].shape[0]
    heads = q_ref.shape[0]
    coming = fetch(parts, buf_ref, in_sems)
    for copy in coming:
        copy.start()
    leaving = []
    for j in range(blocks):
        coming[j].wait()
        for low in range(j * part, (j + 1) * part, 128):
            here = slice(low, low + 128)
            values = buf_ref[here, :].astype(F32)
            scale = lax.rsqrt(jnp.mean(values * values, axis=-1, keepdims=True) + EPS)
            buf_ref[here, :] = (values * scale * gain_ref[...]).astype(BF16)
        rows = pl.ds(j * part, part)
        leaving.append(pltpu.make_async_copy(buf_ref.at[rows], n1_out.at[rows], out_sems.at[j]))
        leaving[-1].start()
        proj = dot(w_ref[...], buf_ref[j * part : (j + 1) * part, :], 1, 1)
        cos = cos_ref[:, j * part : (j + 1) * part][None]
        sin = sin_ref[:, j * part : (j + 1) * part][None]
        there = place(at_ref, j, part)
        cut = heads * HD
        q = rotate(proj[:cut].reshape(heads, HD, part), cos, sin) * SCALE
        q_ref[:, :, there] = q.astype(BF16)
        k = rotate(proj[cut : cut + HD].reshape(1, HD, part), cos, sin)[0]
        v = proj[cut + HD :]
        kt_ref[:, there] = k.astype(BF16)
        vt_ref[:, there] = v.astype(BF16)
        k_ref[there, :] = k.T.astype(BF16)
        v_ref[there, :] = v.T.astype(BF16)
    for copy in leaving:
        copy.wait()


def project(parts, at, gain, w_t, cos, sin, heads):
    blocks = len(parts)
    part, width = parts[0].shape
    full = blocks * part
    if not fits(part):
        cut = heads * HD
        values = jnp.concatenate(parts, axis=0).astype(F32)
        scale = lax.rsqrt(jnp.mean(values * values, axis=-1, keepdims=True) + EPS)
        n1 = (values * scale * gain).astype(BF16)
        proj = dot(w_t, n1, 1, 1)
        q = rotate(proj[:cut].reshape(heads, HD, full), cos[None], sin[None]) * SCALE
        k = rotate(proj[cut : cut + HD].reshape(1, HD, full), cos[None], sin[None])
        both = jnp.concatenate([q.reshape(cut, full), k[0], proj[cut + HD :]], axis=0).astype(BF16)
        both = flip_blocks(both, blocks, True)
        k_t, v_t = both[cut : cut + HD], both[cut + HD :]
        return n1, both[:cut].reshape(heads, HD, full), k_t, v_t, k_t.T, v_t.T
    flat = jax.ShapeDtypeStruct((HD, full), BF16)
    tall = jax.ShapeDtypeStruct((full, HD), BF16)
    return pl.pallas_call(
        functools.partial(project_kernel, blocks),
        in_specs=[IN_SMEM] + [IN_HBM] * blocks + [IN_VMEM] * 4,
        out_specs=[IN_HBM] + [IN_VMEM] * 5,
        out_shape=[
            jax.ShapeDtypeStruct((full, width), BF16),
            jax.ShapeDtypeStruct((heads, HD, full), BF16),
            flat,
            flat,
            tall,
            tall,
        ],
        scratch_shapes=[
            pltpu.VMEM((full, width), BF16),
            pltpu.SemaphoreType.DMA((blocks,)),
            pltpu.SemaphoreType.DMA((blocks,)),
        ],
        compiler_params=PARAMS,
        cost_estimate=SMALL,
    )(at, *parts, gain, w_t, cos, sin)


def merge_kernel(blocks, at_ref, att_ref, w_ref, keep_ref, send_ref):
    part = att_ref.shape[1] // blocks
    for j in range(blocks):
        mine = att_ref[:, place(at_ref, j, part)]
        product = dot(mine, w_ref[...], 0, 0).astype(BF16)
        target, slot = (keep_ref, j) if j < blocks // 2 else (send_ref, j - blocks // 2)
        target[slot * part : (slot + 1) * part, :] = product


def merge_heads(att, at, out_w, blocks):
    cut, full = att.shape
    half = full // 2
    width = out_w.shape[1]
    if not fits(full // blocks):
        product = dot(flip_blocks(att, blocks, False), out_w, 0, 0).astype(BF16)
        return product[:half], product[half:]
    return pl.pallas_call(
        functools.partial(merge_kernel, blocks),
        in_specs=[IN_SMEM, IN_VMEM, IN_VMEM],
        out_specs=[IN_VMEM, IN_VMEM],
        out_shape=[jax.ShapeDtypeStruct((half, width), BF16)] * 2,
        compiler_params=PARAMS,
        cost_estimate=SMALL,
    )(at, att, out_w)


def split_kernel(blocks, has_sum, at_ref, *refs):
    parts = refs[:blocks]
    w_ref, att_ref = refs[blocks : blocks + 2]
    refs = refs[blocks + 2 :]
    if has_sum:
        sum_ref, refs = refs[0], refs[1:]
    grad_ref, delta_ref, wgrad_ref, buf_ref, acc_ref, sems = refs
    part = parts[0].shape[0]
    heads = att_ref.shape[0]
    coming = fetch(parts, buf_ref, sems)
    for copy in coming:
        copy.start()
    for j in range(blocks):
        coming[j].wait()
        rows = buf_ref[j * part : (j + 1) * part, :]
        there = place(at_ref, j, part)
        att = att_ref[:, :, there]
        grad = dot(w_ref[...], rows, 1, 1).astype(BF16).reshape(heads, HD, part)
        grad_ref[:, :, there] = grad
        delta_ref[:, :, there] = jnp.sum(
            grad.astype(F32) * att.astype(F32), axis=1, keepdims=True
        )
        share = jnp.dot(att.reshape(heads * HD, part), rows, preferred_element_type=F32)
        if j:
            acc_ref[...] += share
        elif has_sum:
            acc_ref[...] = sum_ref[...] + share
        else:
            acc_ref[...] = share
    wgrad_ref[...] = acc_ref[...].astype(wgrad_ref.dtype)


def split_heads(parts, at, out_w, att, so_far):
    blocks = len(parts)
    part, width = parts[0].shape
    heads, _, full = att.shape
    kind = F32 if so_far is None else BF16
    if not fits(part):
        rows = jnp.concatenate(parts, axis=0)
        grad = flip_blocks(dot(out_w, rows, 1, 1).astype(BF16), blocks, True)
        grad = grad.reshape(heads, HD, full)
        delta = jnp.sum(grad.astype(F32) * att.astype(F32), axis=1, keepdims=True)
        wgrad = dot(flip_blocks(att.reshape(heads * HD, full), blocks, False), rows, 1, 0)
        return grad, delta, (wgrad if so_far is None else so_far + wgrad).astype(kind)
    more = [] if so_far is None else [so_far]
    return pl.pallas_call(
        functools.partial(split_kernel, blocks, bool(more)),
        in_specs=[IN_SMEM] + [IN_HBM] * blocks + [IN_VMEM] * (2 + len(more)),
        out_specs=[IN_VMEM] * 3,
        out_shape=[
            jax.ShapeDtypeStruct((heads, HD, full), BF16),
            jax.ShapeDtypeStruct((heads, 1, full), F32),
            jax.ShapeDtypeStruct((heads * HD, width), kind),
        ],
        scratch_shapes=[
            pltpu.VMEM((full, width), BF16),
            pltpu.VMEM((heads * HD, width), F32),
            pltpu.SemaphoreType.DMA((blocks,)),
        ],
        compiler_params=PARAMS,
        cost_estimate=SMALL,
    )(at, *parts, out_w, att, *more)


def return_kernel(blocks, has_sum, at_ref, *refs):
    gq_ref, gk_ref, gv_ref, cos_ref, sin_ref, w_ref, n1_in = refs[:7]
    refs = refs[7:]
    if has_sum:
        sum_ref, refs = refs[0], refs[1:]
    keep_ref, send_ref, wgrad_ref, buf_ref, acc_ref, sems = refs
    heads, _, full = gq_ref.shape
    part = full // blocks
    coming = fetch([n1_in.at[pl.ds(j * part, part)] for j in range(blocks)], buf_ref, sems)
    for copy in coming:
        copy.start()
    for j in range(blocks):
        there = place(at_ref, j, part)
        cos = cos_ref[:, j * part : (j + 1) * part][None]
        sin = sin_ref[:, j * part : (j + 1) * part][None]
        gq = rotate_back(gq_ref[:, :, there].astype(F32), cos, sin)
        gk = rotate_back(gk_ref[there, :].T[None], cos, sin)[0]
        grad = jnp.concatenate(
            [
                gq.reshape(heads * HD, part).astype(BF16),
                gk.astype(BF16),
                gv_ref[there, :].T.astype(BF16),
            ],
            axis=0,
        )
        product = dot(grad, w_ref[...], 0, 0).astype(BF16)
        target, slot = (keep_ref, j) if j < blocks // 2 else (send_ref, j - blocks // 2)
        target[slot * part : (slot + 1) * part, :] = product
        coming[j].wait()
        share = jnp.dot(grad, buf_ref[j * part : (j + 1) * part, :], preferred_element_type=F32)
        if j:
            acc_ref[...] += share
        elif has_sum:
            acc_ref[...] = sum_ref[...] + share
        else:
            acc_ref[...] = share
    if has_sum:
        groups, _, columns = wgrad_ref.shape
        for d in range(groups):
            wgrad_ref[d] = acc_ref[:, d * columns : (d + 1) * columns].astype(BF16)
    else:
        wgrad_ref[...] = acc_ref[...]


def return_rows(gq, gk, gv, at, cos, sin, w_t, n1, so_far, groups):
    heads, _, full = gq.shape
    blocks = at.shape[0]
    columns, width = w_t.shape
    half = full // 2
    last = so_far is not None
    if not fits(full // blocks):
        back = jnp.concatenate([gq.reshape(heads * HD, full).astype(F32), gk.T, gv.T], axis=0)
        back = flip_blocks(back, blocks, False)
        turned = rotate_back(
            back[: heads * HD + HD].reshape(heads + 1, HD, full), cos[None], sin[None]
        )
        grad = jnp.concatenate(
            [turned.reshape(heads * HD + HD, full), back[heads * HD + HD :]], axis=0
        ).astype(BF16)
        product = dot(grad, w_t, 0, 0).astype(BF16)
        wgrad = dot(grad, n1, 1, 0)
        if last:
            wgrad = (so_far + wgrad).astype(BF16)
            wgrad = wgrad.reshape(columns, groups, width // groups).transpose(1, 0, 2)
        return product[:half], product[half:], wgrad
    more = [so_far] if last else []
    shape = (groups, columns, width // groups) if last else (columns, width)
    return pl.pallas_call(
        functools.partial(return_kernel, blocks, last),
        in_specs=[IN_SMEM] + [IN_VMEM] * 6 + [IN_HBM] + [IN_VMEM] * len(more),
        out_specs=[IN_VMEM] * 3,
        out_shape=[
            jax.ShapeDtypeStruct((half, width), BF16),
            jax.ShapeDtypeStruct((half, width), BF16),
            jax.ShapeDtypeStruct(shape, BF16 if last else F32),
        ],
        scratch_shapes=[
            pltpu.VMEM((full, width), BF16),
            pltpu.VMEM((columns, width), F32),
            pltpu.SemaphoreType.DMA((blocks,)),
        ],
        compiler_params=PARAMS,
        cost_estimate=SMALL,
    )(at, gq, gk, gv, cos, sin, w_t, n1, *more)


def body(
    tokens,
    cotangent,
    lengths,
    query_weight,
    key_weight,
    value_weight,
    output_weight,
    gate_weight,
    up_weight,
    down_weight,
    attention_gain,
    feed_gain,
):
    seqs, local, width = tokens.shape
    sp = lax.axis_size("sp")
    dp = lax.axis_size("dp")
    me = lax.axis_index("sp")
    full = local * sp
    heads = HEADS // sp
    own_rows = query_weight.shape[0]
    dp_rows = own_rows * sp
    q_cols = heads * HD
    order = order_of(sp)
    hidden = gate_weight.shape[1]

    positions = me * local + jnp.arange(local)
    valid = positions[None, :] < lengths[:, None]

    def pick(array, target):
        head = target * KV // sp
        return array[:, head * HD : (head + 1) * HD]

    extra = jnp.concatenate(
        [attention_gain[:, None], feed_gain[:, None], jnp.zeros((own_rows, 126), BF16)], axis=1
    )
    to_send = jnp.stack(
        [
            jnp.concatenate(
                [
                    query_weight[:, t * q_cols : (t + 1) * q_cols],
                    pick(key_weight, t),
                    pick(value_weight, t),
                    extra,
                ],
                axis=1,
            )
            for t in range(sp)
        ]
    )
    proj_cols = q_cols + 2 * HD
    in_block = lax.all_to_all(to_send, "sp", 0, 0, tiled=True).reshape(dp_rows, proj_cols + 128)
    total = dp * sp
    there = [(n, (n % dp) * sp + n // dp) for n in range(total)]
    back = [(b, a) for a, b in there]
    out_block = lax.ppermute(output_weight, ("dp", "sp"), there)
    out_cols = own_rows * width // dp_rows
    attn_mine = jnp.concatenate([in_block, out_block.reshape(dp_rows, out_cols)], axis=1)
    attn_all = row_major(lax.all_gather(row_major(attn_mine), "dp", axis=0, tiled=True))
    there_is = jnp.isfinite(in_block[0, 0].astype(F32))

    def later(array):
        return jnp.where(there_is, array, jnp.zeros_like(array))

    half = dp // 2
    gu_mine = interleave(gate_weight, up_weight)
    down_t = row_major(lax.all_gather(row_major(down_weight.T), "dp", axis=0, tiled=True))
    gu_w = row_major(
        lax.all_gather(row_major(after(gu_mine, attn_all)), "dp", axis=0, tiled=True)
    )
    held = later(tokens)
    cot_local = jnp.where(valid[..., None], cotangent, jnp.zeros_like(cotangent))
    rows_far = []
    chain = []
    for s in range(seqs):
        rows_far.append(spread(after(held[s], *chain), sp, "sp", 2))
        chain = rows_far[-1][1:]
    rows_all = [spread(far, sp) for far in rows_far]
    cot_far = [spread(after(cot_local[0], *chain), sp, "sp", 2)]
    proj_t = attn_all[:, :proj_cols].T
    gains = attn_all[:, proj_cols : proj_cols + 2].astype(F32)
    gain_one, gain_two = gains[:, 0], gains[:, 1]
    out_w = attn_all[:, proj_cols + 128 :].reshape(q_cols, width)
    rows_all[0][0] = after(rows_all[0][0], *rows_far[-1])

    row_pos = jnp.concatenate([(me ^ member) * local + jnp.arange(local) for member in order])
    frequency = jnp.power(10000.0, -2.0 * jnp.arange(HALF).astype(F32) / HD)
    angles = frequency[:, None] * row_pos.astype(F32)[None, :]
    cos, sin = jnp.cos(angles), jnp.sin(angles)
    at = jnp.stack([me ^ member for member in order]).astype(jnp.int32)

    def norm(values, gain):
        scale = lax.rsqrt(jnp.mean(values * values, axis=-1, keepdims=True) + EPS)
        return values * scale * gain

    def norm_back(grad, values, gain):
        scale = lax.rsqrt(jnp.mean(values * values, axis=-1, keepdims=True) + EPS)
        scaled = grad * gain
        return scale * scaled - values * scale**3 * jnp.mean(scaled * values, axis=-1, keepdims=True)

    normed_one, saved, branches, middles, n2_far, begins = [], [], [], [], [], []

    def take_branch(s, mark):
        branch = after(reduce_far(begins[s], sp), mark)
        middle = tokens[s].astype(F32) + branch
        n2_far.append(spread(norm(middle, gain_two).astype(BF16), sp, "sp", 2))
        branches.append(branch)
        middles.append(middle)

    for s in range(seqs):
        parts = list(rows_all[s])
        if s:
            parts[0] = after(parts[0], begins[-1])
        n1, q, k_t, v_t, k, v = project(parts, at, gain_one[None], proj_t, cos, sin, heads)
        normed_one.append(n1)
        att, lse = attend_forward(q, k, v_t, lengths[s : s + 1])
        flat = att.reshape(q_cols, full)
        if s == 0:
            flat = after(flat, *cot_far[0], down_t)
        else:
            take_branch(s - 1, att)
        begins.append(reduce_pair(*merge_heads(flat, at, out_w, sp), sp))
        saved.append((q, k, k_t, v, att, lse))
    for s in range(1, seqs):
        cot_far.append(spread(after(cot_local[s], begins[-1]), sp, "sp", 2))
    cot_parts = [spread(far, sp) for far in cot_far]
    first = [after(part, begins[-1], *n2_far[0]) for part in cot_parts[0]]
    hidden_grads, cot_all = [[member] for member in hidden_grad(first, down_t)]
    gu_w = after(gu_w, hidden_grads[0])
    take_branch(seqs - 1, gu_w)
    begun = begins[-1]
    normed_two = [spread(n2_far[0], sp)]

    def mlp_near(hid):
        return reduce_near(lambda lo, hi: dot(hid[lo:hi], down_t, 1, 1), full, sp)

    begun_mixed = []
    hiddens, gu_grads, n2_grads, middle_grads, grad_rows = [], [], [], [], []
    down_wgrad = 0.0
    for s in range(seqs):
        n2 = [after(part, begun, hidden_grads[s]) for part in normed_two[s]]
        hid, gu_grad, joined = feed(n2, gu_w, hidden_grads[s])
        normed_two[s] = joined
        hiddens.append(hid)
        gu_grads.append(gu_grad)
        if s < seqs - 1:
            low, high = [n2_far[s + 1][0]], n2_far[s + 1]
            parts = [after(part, gu_grad, *low) for part in cot_parts[s + 1]]
            for array, made in zip((hidden_grads, cot_all), hidden_grad(parts, down_t)):
                array.append(made)
            hid = after(hid, *low)
            down_wgrad = row_major(dot(cot_all[s], hid, 0, 0))
            begun_mixed.append(mlp_near(hid))
            high = high + [down_wgrad, begun_mixed[0]]
        else:
            low, high = [n2_grads[0]], [n2_grads[0]]
        send, keep = after(gu_grad, *low), after(gu_grad, *high)
        begun = reduce_near(
            lambda lo, hi: dot((keep if lo == 0 else send)[lo:hi], gu_w, 1, 1), full, sp
        )
        n2_grads.append(reduce_far(begun, sp))
        if s < seqs - 1:
            normed_two.append(spread(n2_far[s + 1], sp))
    gu_wgrad = 0.0
    for s in range(seqs):
        held = after(n2_grads[s], gu_grads[-1]) if s == 0 else after(n2_grads[s], gu_wgrad)
        middle_grads.append(cot_local[s].astype(F32) + norm_back(held, middles[s], gain_two))
        parts = spread(middle_grads[s].astype(BF16), sp, "sp", 2)
        far_rows = parts[1:]
        if s == 0:
            gu_wgrad = dot(after(normed_two[0], begun, middle_grads[0]), gu_grads[0], 0, 0)
            parts = [after(part, gu_wgrad) for part in parts]
        grad_rows.append(spread(parts, sp))
        if s == 0:
            for t in range(1, seqs):
                gu_wgrad = gu_wgrad + dot(after(normed_two[t], *grad_rows[0]), gu_grads[t], 0, 0)
            gu_wgrad = gu_wgrad.astype(BF16)
    rows = after(cot_all[-1], middle_grads[-1])
    down_wgrad = down_wgrad + dot(rows, hiddens[-1], 0, 0)
    down_wgrad = down_wgrad.astype(BF16)
    hid = after(hiddens[-1], down_wgrad, *far_rows)
    begun_mixed.append(mlp_near(hid))

    feed_wgrad = jnp.concatenate([gu_wgrad, down_wgrad], axis=1)
    feed_grad = row_major(
        lax.psum_scatter(row_major(feed_wgrad), "dp", scatter_dimension=0, tiled=True)
    )

    def norm_sums(mixed):
        sums = jnp.stack(
            [
                jnp.stack(
                    [
                        jnp.sum(jnp.where(valid[s][:, None], member[s] * member[s], 0.0))
                        for s in range(seqs)
                    ]
                )
                for member in ([tokens[s].astype(F32) for s in range(seqs)], branches, mixed)
            ]
        )
        return sums

    proj_wgrad = None
    out_wgrad = None
    input_grads = []
    for s in range(seqs):
        q, k, k_t, v, att, lse = saved[s]
        rows = list(grad_rows[s])
        rows[0] = after(rows[0], mark) if s else after(rows[0], *begun_mixed)
        att_grad, delta, out_wgrad = split_heads(rows, at, out_w, att, out_wgrad)
        if s:
            q = after(q, begun)
            staying, got = halve(blocks_of(out_wgrad, dp), 1, dp)
        gq, gk, gv = attend_backward(q, att_grad, k, k_t, v, lse, delta, lengths[s : s + 1])
        mark = gq
        if s == 0:
            mixed = [reduce_far(after(begun_mixed[0], *far_rows), sp)]
            gq = after(gq, mixed[0])
            mixed += [reduce_far(after(begun_mixed[t], mark), sp) for t in range(1, seqs)]
        else:
            sums = norm_sums(mixed)
            gq = after(gq, got, *mixed, n1_grad)
        keep, send, proj_wgrad = return_rows(
            gq, gk, gv, at, cos, sin, proj_t, normed_one[s], proj_wgrad, dp
        )
        begun = reduce_pair(keep, send, sp)
        if s == 0:
            n1_grad = reduce_far(begun, sp)
        else:
            out_left = join(staying, after(got, mark)).astype(BF16)
            out_staying, out_got = halve(out_left, 2, dp)
            n1_grad = reduce_far(begun, sp)
        rest = norm_back(n1_grad, tokens[s].astype(F32), gain_one)
        input_grads.append((middle_grads[s] + rest).astype(BF16))
    input_grad = jnp.stack(input_grads)
    staying, got = halve(proj_wgrad, 1, dp)
    left = join(staying, after(got, begun)).astype(BF16)
    out_left = join(out_staying, after(out_got, left)).astype(BF16)
    staying, got = halve(left, 2, dp)
    left = join(staying, after(got, n1_grad, feed_grad)).astype(BF16)
    proj_grad = finish(left, 4, dp)
    out_grad = finish(after(out_left, left), 4, dp)
    out_grad = lax.ppermute(out_grad.astype(BF16), ("dp", "sp"), back).astype(F32)
    feed_grad = after(feed_grad, left).astype(F32)
    gate_out, up_out = separate(feed_grad[:, : 2 * hidden])
    down_out = feed_grad[:, 2 * hidden :].T

    block_out = jnp.stack(
        [((middles[s] + mixed[s]) * valid[s][:, None]).astype(BF16) for s in range(seqs)]
    )
    proj_grad = proj_grad.astype(BF16).reshape(proj_cols, sp, own_rows).transpose(1, 0, 2)
    proj_grad = lax.all_to_all(proj_grad, "sp", 0, 0, tiled=True).astype(F32)
    query_grad = proj_grad[:, :q_cols].transpose(2, 0, 1).reshape(own_rows, HEADS * HD)

    def kv_grad(array):
        copies = array.reshape(KV, sp // KV, HD, own_rows).sum(axis=1)
        return copies.transpose(2, 0, 1).reshape(own_rows, KV * HD)

    key_grad = kv_grad(proj_grad[:, q_cols : q_cols + HD])
    value_grad = kv_grad(proj_grad[:, q_cols + HD :])

    def rowwise(weight, grad):
        return jnp.sum(weight.astype(F32) * grad, axis=1)

    gain_one_grad = (
        rowwise(query_weight, query_grad)
        + rowwise(key_weight, key_grad)
        + rowwise(value_weight, value_grad)
    ) / attention_gain.astype(F32)
    shares = rowwise(gate_weight, gate_out) + rowwise(up_weight, up_out)
    gain_two_grad = finish(blocks_of(shares, sp), 1, sp, "sp") / feed_gain.astype(F32)

    sums = after(sums, n1_grad)
    bit = 1
    while bit < sp:
        sums = sums + swap(sums, bit, sp)
        bit *= 2
    branch_norms = jnp.sqrt(sums / (lengths.astype(F32) * width))
    return (
        block_out,
        input_grad,
        query_grad,
        key_grad,
        value_grad,
        out_grad,
        gate_out,
        up_out,
        down_out,
        gain_one_grad,
        gain_two_grad,
        branch_norms,
    )


def solution(mesh):
    rows = P(("dp", "sp"), None)
    gain = P(("dp", "sp"))
    seq = P("dp", "sp", None)
    in_specs = (
        seq, seq, P("dp"), rows, rows, rows, rows,
        P("dp", "sp"), P("dp", "sp"), P("sp", "dp"), gain, gain,
    )
    out_specs = (
        seq, seq, rows, rows, rows, rows,
        P("dp", "sp"), P("dp", "sp"), P("sp", "dp"), gain, gain, P(None, "dp"),
    )
    return jax.shard_map(body, mesh=mesh, in_specs=in_specs, out_specs=out_specs, check_vma=False)
```
